512 devices in a mesh: row: 32 (over z_hi, y, core), col: 16 (over z_lo, x).
Axes of the slice: x: 4, y: 8, z: 8 (z_hi: 2, z_lo: 4; z = z_hi * 4 + z_lo), core: 2. Of those that a mesh axis runs over, the one named last changes fastest.
Arguments:
- pair_rep: bfloat16 [1024, 1024, 128], P('row', 'col'), may hold values from -6 to 6
- in_gain: float32 [2, 128], replicated, may hold values from 0.1 to 1.9
- in_bias: float32 [2, 128], replicated, may hold values from -3 to 3
- proj_w: bfloat16 [2, 128, 512], replicated, may hold values from -0.5 to 0.5
- gate_w: bfloat16 [2, 128, 128], replicated, may hold values from -0.5 to 0.5
- out_gain: float32 [2, 128], replicated, may hold values from 0.1 to 1.9
- out_bias: float32 [2, 128], replicated, may hold values from -3 to 3
- out_w: bfloat16 [2, 128, 128], replicated, may hold values from -0.5 to 0.5
Outputs:
- pair_out: bfloat16 [1024, 1024, 128], P('row', 'col')
The draws below stay inside these ranges and needn't reach their ends.
All inputs are finite; a program needn't handle non-finite values.
Results may differ from the reference program's by a relative error of at most 0.007.
Values may be sent and summed in bfloat16 or wider, within the bound.
No kernel may reach another device: no remote copies, remote signals or barrier semaphores. Data moves between devices by JAX's collectives and lax.ppermute only.
A program may use at most 64 MiB of HBM per device.

```python
import jax
import jax.numpy as jnp
from jax import lax

D = 128
CH = 128
N = 1024


def steps_of(stream_key, dims, split, smallest, top_value):
    def one(dim, shards_of):
        heights = jax.random.uniform(jax.random.fold_in(jax.random.fold_in(stream_key, 6), dim), (shards_of,), jnp.float32, smallest / len(split), top_value / len(split))
        return jnp.repeat(jnp.exp(heights), dims[dim] // shards_of).reshape((-1,) + (1,) * (len(dims) - dim - 1))

    level = one(*split[0])
    for cut in split[1:]:
        level = level * one(*cut)
    return level


def gaussian(key, dims, scale, reach, shards=(), dtype=jnp.bfloat16):
    drawn = scale * jax.random.normal(key, dims, jnp.float32)
    if shards:
        drawn = drawn * steps_of(key, dims, shards, -0.22, 0.18)
    return jnp.clip(drawn, -reach, reach).astype(dtype)


def setup_inputs(seed: int = 0) -> dict:
    streams_of = jax.random.split(jax.random.key(seed), 9)
    return {
        "pair_rep": gaussian(streams_of[0], (N, N, D), 1.0, 6.0, ((0, 32), (1, 16))),
        "in_gain": jnp.clip(1.0 + 0.18 * jax.random.normal(streams_of[1], (2, D), jnp.float32), 0.1, 1.9),
        "in_bias": gaussian(streams_of[2], (2, D), 0.5, 3.0, (), jnp.float32),
        "proj_w": gaussian(streams_of[3], (2, D, 4 * CH), D ** -0.5, 0.5),
        "gate_w": gaussian(streams_of[4], (2, D, D), D ** -0.5, 0.5),
        "out_gain": jnp.clip(1.0 + 0.18 * jax.random.normal(streams_of[5], (2, CH), jnp.float32), 0.1, 1.9),
        "out_bias": gaussian(streams_of[6], (2, CH), 0.5, 3.0, (), jnp.float32),
        "out_w": gaussian(streams_of[7], (2, CH, D), CH ** -0.5, 0.5),
    }


def norm_cells(values, gain, bias):
    center = values - lax.optimization_barrier(jnp.mean(values, axis=-1, keepdims=True))
    spread = lax.optimization_barrier(jnp.mean(center * center, axis=-1, keepdims=True))
    return center * lax.rsqrt(spread + 1e-05) * gain + bias

def one_update(pair_rep, layer_index, outgoing, in_gain, in_bias, proj_w, gate_w, out_gain, out_bias, out_w):
    flat_pair = pair_rep.reshape(N * N, D).astype(jnp.float32)
    normed = norm_cells(flat_pair, in_gain[layer_index], in_bias[layer_index]).astype(jnp.bfloat16)
    halves = jnp.dot(normed, proj_w[layer_index], preferred_element_type=jnp.float32)
    left_op = (jax.nn.sigmoid(halves[:, CH:2 * CH]) * halves[:, :CH]).astype(jnp.bfloat16)
    right_op = (jax.nn.sigmoid(halves[:, 3 * CH:]) * halves[:, 2 * CH:3 * CH]).astype(jnp.bfloat16)
    gate = jax.nn.sigmoid(jnp.dot(normed, gate_w[layer_index], preferred_element_type=jnp.float32))
    left_cube = left_op.astype(jnp.float32).reshape(N, N, CH).transpose(2, 0, 1)
    right_cube = right_op.astype(jnp.float32).reshape(N, N, CH).transpose(2, 0, 1)
    if outgoing:
        tri = jnp.einsum('cik,cjk->cij', left_cube, right_cube, precision=lax.Precision.HIGHEST)
    else:
        tri = jnp.einsum('cki,ckj->cij', left_cube, right_cube, precision=lax.Precision.HIGHEST)
    tri = tri.astype(jnp.bfloat16).transpose(1, 2, 0).reshape(N * N, CH).astype(jnp.float32)
    mixed = norm_cells(tri, out_gain[layer_index], out_bias[layer_index]).astype(jnp.bfloat16)
    delta = gate * jnp.dot(mixed, out_w[layer_index], preferred_element_type=jnp.float32)
    return (flat_pair + delta).astype(jnp.bfloat16).reshape(N, N, D)

def reference(pair_rep, in_gain, in_bias, proj_w, gate_w, out_gain, out_bias, out_w):
    middle = one_update(pair_rep, 0, True, in_gain, in_bias, proj_w, gate_w, out_gain, out_bias, out_w)
    return one_update(middle, 1, False, in_gain, in_bias, proj_w, gate_w, out_gain, out_bias, out_w)
```

```python
import functools

import jax
import jax.numpy as jnp
from jax import lax
from jax.experimental import pallas as pl
from jax.experimental.pallas import tpu as pltpu
from jax.sharding import Mesh
from jax.sharding import PartitionSpec as P

GROUP = ("zhi", "y", "core", "zlo")
EPS = 1e-05
F32 = jnp.float32
BF16 = jnp.bfloat16


def _params(mib):
    return pltpu.CompilerParams(vmem_limit_bytes=mib << 20)


def _norm(values, axis, gain, bias):
    center = values - jnp.mean(values, axis=axis, keepdims=True)
    spread = jnp.mean(center * center, axis=axis, keepdims=True)
    return center * lax.rsqrt(spread + EPS) * gain + bias


def _project(cells, gain, bias, turned_w, gate_w):
    normed = _norm(cells, 1, gain, bias).astype(BF16)
    halves = lax.dot_general(
        turned_w, normed, (((1,), (1,)), ((), ())), preferred_element_type=F32
    )
    left = jax.nn.sigmoid(halves[128:256]) * halves[:128]
    right = jax.nn.sigmoid(halves[384:]) * halves[256:384]
    gate = jax.nn.sigmoid(jnp.dot(normed, gate_w, preferred_element_type=F32))
    return left, right, gate


def _rows(ref, s):
    return jnp.concatenate([ref[s], ref[16 + s]], axis=0)


def _put_rows(ref, s, value):
    ref[s] = value[:64]
    ref[16 + s] = value[64:]


def _first_kernel(p_ref, gain_ref, bias_ref, w_ref, gw_ref, out_ref, gate_ref, scr):
    turned_w = w_ref[...].T
    for s in range(16):
        cells = _rows(p_ref, s).astype(F32)
        left, right, gate = _project(cells, gain_ref[...], bias_ref[...], turned_w, gw_ref[...])
        scr[pl.ds(s, 128, stride=32), :] = left
        scr[pl.ds(16 + s, 128, stride=32), :] = right
        _put_rows(gate_ref, s, gate)
    out_ref[...] = scr[...].astype(BF16)


def _finished(scr, s, cells, gate, gain, bias, out_w):
    tri = scr[pl.ds(s, 128, stride=16), :]
    mixed = _norm(tri, 0, gain, bias).astype(BF16)
    projected = lax.dot_general(
        mixed, out_w, (((0,), (0,)), ((), ())), preferred_element_type=F32
    )
    return (cells + gate * projected).astype(BF16)


def _middle_kernel(
    t_ref, p_ref, g_ref, og_ref, ob_ref, ow_ref, gain_ref, bias_ref, w_ref, gw_ref,
    mid_ref, left_ref, right_ref, gate_ref, tri_scr, left_scr, right_scr,
):
    tri_scr[...] = t_ref[...].astype(F32)
    turned_w = w_ref[...].T
    for s in range(16):
        cells = _rows(p_ref, s).astype(F32)
        mid = _finished(tri_scr, s, cells, _rows(g_ref, s), og_ref[...], ob_ref[...], ow_ref[...])
        _put_rows(mid_ref, s, mid)
        left, right, gate = _project(
            mid.astype(F32), gain_ref[...], bias_ref[...], turned_w, gw_ref[...]
        )
        left_scr[pl.ds(s, 128, stride=16), :] = left
        right_scr[pl.ds(s, 128, stride=16), :] = right
        _put_rows(gate_ref, s, gate)
    left_ref[...] = left_scr[...].astype(BF16)
    right_ref[...] = right_scr[...].astype(BF16)


def _last_kernel(t_ref, p_ref, g_ref, og_ref, ob_ref, ow_ref, out_ref, tri_scr):
    tri_scr[...] = t_ref[...].astype(F32)
    for s in range(16):
        cells = _rows(p_ref, s).astype(F32)
        out = _finished(tri_scr, s, cells, _rows(g_ref, s), og_ref[...], ob_ref[...], ow_ref[...])
        _put_rows(out_ref, s, out)


def _pair_up(one, two):
    low = jnp.concatenate([one[..., :64], two[..., :64]], axis=-1)
    high = jnp.concatenate([one[..., 64:], two[..., 64:]], axis=-1)
    return low, high


def _outgoing_kernel(x_ref, in_ref, out_ref, l_scr, r_scr):
    for t, scr in ((0, l_scr), (1, r_scr)):
        for pair in range(2):
            low, high = _pair_up(in_ref[:, 2 * pair, t], in_ref[:, 2 * pair + 1, t])
            scr[:, 0, :, pair * 128 : pair * 128 + 128] = low
            scr[:, 1, :, pair * 128 : pair * 128 + 128] = high
    right = r_scr[...].reshape(1024, 256)
    here = x_ref[0]
    for part in range(4):
        left = l_scr[part * 8 : part * 8 + 8].reshape(256, 256)
        tri = lax.dot_general(left, right, (((1,), (1,)), ((), ())), preferred_element_type=F32)
        tri = tri.astype(BF16).reshape(8, 2, 16, 1024)
        for zlo in range(4):
            for pair in range(2):
                lanes = tri[..., zlo * 256 + pair * 128 : zlo * 256 + pair * 128 + 128]
                low, high = _pair_up(lanes[:, 0], lanes[:, 1])
                rows = slice(part * 8, part * 8 + 8)
                out_ref[(2 * pair - here) & 3, rows, zlo] = low
                out_ref[(2 * pair + 1 - here) & 3, rows, zlo] = high


def _incoming_kernel(
    x_ref, own_ref, before_ref, after_ref, far_a_ref, far_b_ref, r_ref, out_ref, l_scr, r_scr
):
    def load(scr, parts):
        base = 0
        for ref in parts:
            n = ref.shape[0]
            for pair in range(2):
                low, high = _pair_up(ref[:, 2 * pair], ref[:, 2 * pair + 1])
                lanes = slice(pair * 128, pair * 128 + 128)
                scr[0, base : base + n, :, lanes] = low
                scr[1, base : base + n, :, lanes] = high
            base += n

    load(r_scr, (r_ref,))
    right = r_scr[...].reshape(1024, 256)
    here = x_ref[0]
    for step, parts in ((0, (own_ref,)), (3, (before_ref,)), (1, (after_ref,)), (2, (far_a_ref, far_b_ref))):
        load(l_scr, parts)
        left = l_scr[...].reshape(1024, 256)
        tri = lax.dot_general(left, right, (((0,), (0,)), ((), ())), preferred_element_type=F32)
        tri = tri.astype(BF16).reshape(4, 2, 2, 16, 256)
        for pair in range(2):
            lanes = tri[..., pair * 128 : pair * 128 + 128]
            low, high = _pair_up(lanes[:, :, 0], lanes[:, :, 1])
            out_ref[:, (here + step) & 3, :, 2 * pair] = low
            out_ref[:, (here + step) & 3, :, 2 * pair + 1] = high


def _call(kernel, outs, scratch, args, mib=48, scalar=False):
    specs = [pl.BlockSpec(memory_space=pltpu.VMEM) for _ in args]
    if scalar:
        specs[0] = pl.BlockSpec(memory_space=pltpu.SMEM)
    return pl.pallas_call(
        kernel,
        out_shape=[jax.ShapeDtypeStruct(shape, dtype) for shape, dtype in outs],
        in_specs=specs,
        out_specs=[pl.BlockSpec(memory_space=pltpu.VMEM) for _ in outs],
        scratch_shapes=[pltpu.VMEM(shape, dtype) for shape, dtype in scratch],
        compiler_params=_params(mib),
    )(*args)


def _exchange(tiles):
    return lax.all_to_all(tiles, GROUP, split_axis=0, concat_axis=0, tiled=True)


def _shift(value, step):
    return lax.ppermute(value, "x", [(i, (i + step) % 4) for i in range(4)])


def _sum(*parts):
    total = parts[0].astype(F32)
    for part in parts[1:]:
        total = total + part.astype(F32)
    return total.astype(BF16)


def body(pair_rep, in_gain, in_bias, proj_w, gate_w, out_gain, out_bias, out_w):
    block = pair_rep.shape
    here = lax.axis_index("x").astype(jnp.int32).reshape(1)

    def row_of(value, u):
        return value[u].reshape(1, 128)

    def column_of(value, u):
        return value[u].reshape(128, 1)

    tiles, gate = _call(
        _first_kernel,
        [((4096, 128), BF16), (block, F32)],
        [((4096, 128), F32)],
        (pair_rep, row_of(in_gain, 0), row_of(in_bias, 0), proj_w[0], gate_w[0]),
    )
    both = _exchange(tiles.reshape(128, 32, 128)).reshape(32, 4, 2, 16, 128)
    (partial,) = _call(
        _outgoing_kernel,
        [((4, 32, 4, 16, 128), BF16)],
        [((32, 2, 16, 256), BF16), ((32, 2, 16, 256), BF16)],
        (here, both),
        scalar=True,
    )
    far_up = _shift(partial[2, :16], 1)
    far_down = _shift(partial[2, 16:], -1)
    up = jnp.concatenate([_sum(partial[1, :16], far_up), partial[1, 16:]], axis=0)
    down = jnp.concatenate([partial[3, :16], _sum(partial[3, 16:], far_down)], axis=0)
    tri = _sum(partial[0], _shift(up, 1), _shift(down, -1))
    tri = _exchange(tri.reshape(128, 16, 128))

    middle, left, right, gate = _call(
        _middle_kernel,
        [(block, BF16), ((2048, 128), BF16), ((2048, 128), BF16), (block, F32)],
        [((2048, 128), F32), ((2048, 128), F32), ((2048, 128), F32)],
        (
            tri.reshape(2048, 128), pair_rep, gate,
            column_of(out_gain, 0), column_of(out_bias, 0), out_w[0],
            row_of(in_gain, 1), row_of(in_bias, 1), proj_w[1], gate_w[1],
        ),
    )
    left = _exchange(left.reshape(128, 16, 128))
    left, right = lax.optimization_barrier((left, right))
    right = _exchange(right.reshape(128, 16, 128)).reshape(32, 4, 16, 128)
    left = left.reshape(32, 4, 16, 128)
    before = _shift(left, 1)
    after = _shift(left, -1)
    far_a = _shift(before[:16], 1)
    far_b = _shift(after[16:], -1)
    (tri,) = _call(
        _incoming_kernel,
        [((4, 4, 2, 4, 16, 128), BF16)],
        [((2, 32, 16, 256), BF16), ((2, 32, 16, 256), BF16)],
        (here, left, before, after, far_a, far_b, right),
        scalar=True,
    )
    tri = _exchange(tri.reshape(128, 16, 128))
    (out,) = _call(
        _last_kernel,
        [(block, BF16)],
        [((2048, 128), F32)],
        (
            tri.reshape(2048, 128), middle, gate,
            column_of(out_gain, 1), column_of(out_bias, 1), out_w[1],
        ),
    )
    return out


def solution(mesh):
    fine = Mesh(mesh.devices.reshape(2, 8, 2, 4, 4), ("zhi", "y", "core", "zlo", "x"))
    cells = P(("zhi", "y", "core"), ("zlo", "x"), None)
    placed = (cells, P(), P(), P(), P(), P(), P(), P())
    return jax.shard_map(body, mesh=fine, in_specs=placed, out_specs=cells, check_vma=False)
```

```python
import jax
import jax.numpy as jnp
from jax import lax
from jax.experimental import pallas as pl
from jax.experimental.pallas import tpu as pltpu
from jax.sharding import Mesh
from jax.sharding import PartitionSpec as P

GROUP = ("zhi", "y", "zlo", "x")
EPS = 1e-05
F32 = jnp.float32
BF16 = jnp.bfloat16


def _norm(values, axis, gain, bias):
    center = values - jnp.mean(values, axis=axis, keepdims=True)
    spread = jnp.mean(center * center, axis=axis, keepdims=True)
    return center * lax.rsqrt(spread + EPS) * gain + bias


def _project(cells, gain, bias, turned_w, gate_w):
    normed = _norm(cells, 1, gain, bias).astype(BF16)
    halves = lax.dot_general(
        turned_w, normed, (((1,), (1,)), ((), ())), preferred_element_type=F32
    )
    left = jax.nn.sigmoid(halves[128:256]) * halves[:128]
    right = jax.nn.sigmoid(halves[384:]) * halves[256:384]
    gate = jax.nn.sigmoid(jnp.dot(normed, gate_w, preferred_element_type=F32))
    return left, right, gate


def _pair_up(one, two):
    low = jnp.concatenate([one[..., :64], two[..., :64]], axis=-1)
    high = jnp.concatenate([one[..., 64:], two[..., 64:]], axis=-1)
    return low, high


def _quarter(parts, q):
    return jnp.concatenate([part[..., 32 * q : 32 * q + 32] for part in parts], axis=-1)


def _rows(ref, s):
    return jnp.concatenate([ref[s], ref[16 + s]], axis=0)


def _put_rows(ref, s, value):
    ref[s] = value[:64]
    ref[16 + s] = value[64:]


def _put_operands(scr, s, left, right):
    low, high = _pair_up(left, right)
    scr[pl.ds(s, 128, stride=32), :] = low
    scr[pl.ds(16 + s, 128, stride=32), :] = high


def _column(ref, u):
    return jnp.broadcast_to(ref[u : u + 1, :], (128, 128)).T


def _first_kernel(p_ref, gain_ref, bias_ref, w_ref, gw_ref, out_ref, gate_ref, scr):
    turned_w = w_ref[0].T
    for s in range(16):
        cells = jnp.concatenate(
            [p_ref[s, :32], p_ref[16 + s, :32], p_ref[s, 32:], p_ref[16 + s, 32:]], axis=0
        ).astype(F32)
        left, right, gate = _project(cells, gain_ref[:1], bias_ref[:1], turned_w, gw_ref[0])
        _put_operands(scr, s, left, right)
        gate_ref[s, :32] = gate[:32]
        gate_ref[16 + s, :32] = gate[32:64]
        gate_ref[s, 32:] = gate[64:96]
        gate_ref[16 + s, 32:] = gate[96:]
    out_ref[...] = scr[...].astype(BF16)


def _load_products(t_ref, scr):
    total = t_ref[:, 0].astype(F32) + t_ref[:, 1].astype(F32)
    scr[...] = total.reshape(2048, 128)


def _finished(scr, s, cells, gate, gain, bias, out_w):
    tri = scr[pl.ds(s, 128, stride=16), :]
    mixed = _norm(tri, 0, gain, bias).astype(BF16)
    projected = lax.dot_general(
        mixed, out_w, (((0,), (0,)), ((), ())), preferred_element_type=F32
    )
    return (cells + gate * projected).astype(BF16)


def _middle_kernel(
    t_ref, p_ref, g_ref, og_ref, ob_ref, ow_ref, gain_ref, bias_ref, w_ref, gw_ref,
    mid_ref, out_ref, gate_ref, tri_scr, scr,
):
    _load_products(t_ref, tri_scr)
    turned_w = w_ref[1].T
    out_gain, out_bias = _column(og_ref, 0), _column(ob_ref, 0)
    for s in range(16):
        cells = _rows(p_ref, s).astype(F32)
        mid = _finished(tri_scr, s, cells, _rows(g_ref, s), out_gain, out_bias, ow_ref[0])
        _put_rows(mid_ref, s, mid)
        left, right, gate = _project(
            mid.astype(F32), gain_ref[1:], bias_ref[1:], turned_w, gw_ref[1]
        )
        _put_operands(scr, s, left, right)
        _put_rows(gate_ref, s, gate)
    out_ref[...] = scr[...].astype(BF16)


def _last_kernel(t_ref, p_ref, g_ref, og_ref, ob_ref, ow_ref, out_ref, tri_scr):
    _load_products(t_ref, tri_scr)
    out_gain, out_bias = _column(og_ref, 1), _column(ob_ref, 1)
    for s in range(16):
        cells = _rows(p_ref, s).astype(F32)
        out = _finished(tri_scr, s, cells, _rows(g_ref, s), out_gain, out_bias, ow_ref[1])
        _put_rows(out_ref, s, out)


def _put_products(out_ref, rows, tri):
    tri = tri.astype(BF16).reshape(-1, 2, 16, 1024)
    for pair in range(8):
        lanes = tri[..., pair * 128 : pair * 128 + 128]
        low, high = _pair_up(lanes[:, 0], lanes[:, 1])
        out_ref[rows, 2 * pair] = low
        out_ref[rows, 2 * pair + 1] = high


def _outgoing_kernel(core_ref, own_ref, other_ref, out_ref, l_scr, r_scr):
    core = core_ref[0]
    for zlo in range(4):
        lanes = slice(zlo * 128, zlo * 128 + 128)
        own = [own_ref[:, zlo * 4 + x] for x in range(4)]
        other = [other_ref[:, zlo * 4 + x] for x in range(4)]
        for b in range(2):
            l_scr[:, b, :, lanes] = _quarter(own, b)
            r_scr[:, pl.ds(core, 1), b, :, lanes] = _quarter(own, 2 + b)[:, None]
            r_scr[:, pl.ds(1 - core, 1), b, :, lanes] = _quarter(other, 2 + b)[:, None]
    right = r_scr[...].reshape(1024, 512)
    for part in range(2):
        rows = slice(part * 8, part * 8 + 8)
        left = l_scr[rows].reshape(256, 512)
        tri = lax.dot_general(left, right, (((1,), (1,)), ((), ())), preferred_element_type=F32)
        _put_products(out_ref, rows, tri)


def _incoming_kernel(core_ref, own_ref, other_ref, out_ref, l_scr, r_scr):
    first = core_ref[0] == 0
    for at, ref in ((0, own_ref), (1, other_ref)):
        for zlo in range(4):
            parts = [ref[:, zlo * 4 + x] for x in range(4)]
            lanes = slice(zlo * 128, zlo * 128 + 128)
            l_scr[at, :, :, lanes] = jnp.where(first, _quarter(parts, 0), _quarter(parts, 1))
            for pair in range(2):
                _, high = _pair_up(parts[2 * pair], parts[2 * pair + 1])
                start = zlo * 256 + pair * 128
                r_scr[at, :, :, start : start + 128] = high
    right = r_scr[...].reshape(512, 1024)
    for part in range(2):
        left = l_scr[:, :, :, part * 256 : part * 256 + 256].reshape(512, 256)
        tri = lax.dot_general(left, right, (((0,), (0,)), ((), ())), preferred_element_type=F32)
        _put_products(out_ref, slice(part * 8, part * 8 + 8), tri)


def _call(kernel, outs, scratch, args, scalar=False):
    specs = [pl.BlockSpec(memory_space=pltpu.VMEM) for _ in args]
    if scalar:
        specs[0] = pl.BlockSpec(memory_space=pltpu.SMEM)
    return pl.pallas_call(
        kernel,
        out_shape=[jax.ShapeDtypeStruct(shape, dtype) for shape, dtype in outs],
        in_specs=specs,
        out_specs=[pl.BlockSpec(memory_space=pltpu.VMEM) for _ in outs],
        scratch_shapes=[pltpu.VMEM(shape, dtype) for shape, dtype in scratch],
        compiler_params=pltpu.CompilerParams(vmem_limit_bytes=40 << 20),
    )(*args)


def _exchange(tiles):
    return lax.all_to_all(
        tiles.reshape(256, 16, 128), GROUP, split_axis=0, concat_axis=0, tiled=True
    )


def _products(kernel, scratch, tiles, core):
    own = _exchange(tiles).reshape(16, 16, 16, 128)
    other = lax.ppermute(own, "core", [(0, 1), (1, 0)])
    (out,) = _call(
        kernel, [((16, 16, 16, 128), BF16)], scratch, (core, own, other), scalar=True
    )
    return _exchange(out).reshape(128, 2, 16, 128)


def body(pair_rep, in_gain, in_bias, proj_w, gate_w, out_gain, out_bias, out_w):
    block = pair_rep.shape
    core = lax.axis_index("core").astype(jnp.int32).reshape(1)
    tiles, gate = _call(
        _first_kernel,
        [((4096, 128), BF16), (block, F32)],
        [((4096, 128), F32)],
        (pair_rep, in_gain, in_bias, proj_w, gate_w),
    )
    tri = _products(
        _outgoing_kernel,
        [((16, 2, 16, 512), BF16), ((16, 2, 2, 16, 512), BF16)],
        tiles,
        core,
    )
    middle, tiles, gate = _call(
        _middle_kernel,
        [(block, BF16), ((4096, 128), BF16), (block, F32)],
        [((2048, 128), F32), ((4096, 128), F32)],
        (tri, pair_rep, gate, out_gain, out_bias, out_w, in_gain, in_bias, proj_w, gate_w),
    )
    tri = _products(
        _incoming_kernel,
        [((2, 16, 16, 512), BF16), ((2, 16, 16, 1024), BF16)],
        tiles,
        core,
    )
    (out,) = _call(
        _last_kernel,
        [(block, BF16)],
        [((2048, 128), F32)],
        (tri, middle, gate, out_gain, out_bias, out_w),
    )
    return out


def solution(mesh):
    fine = Mesh(mesh.devices.reshape(2, 8, 2, 4, 4), ("zhi", "y", "core", "zlo", "x"))
    cells = P(("zhi", "y", "core"), ("zlo", "x"), None)
    placed = (cells, P(), P(), P(), P(), P(), P(), P())
    return jax.shard_map(body, mesh=fine, in_specs=placed, out_specs=cells, check_vma=False)
```

```python
import jax
import jax.numpy as jnp
from jax import lax
from jax.experimental import pallas as pl
from jax.experimental.pallas import tpu as pltpu
from jax.sharding import Mesh
from jax.sharding import PartitionSpec as P

OUTGOING = ("zhi", "y", "zlo", "xlo")
INCOMING = ("y", "zlo", "xhi", "xlo")
EPS = 1e-05
F32 = jnp.float32
BF16 = jnp.bfloat16

OPERAND_STEP = 40
PRODUCT_STEP = 24
OPERAND_SCRATCH = ((128 * OPERAND_STEP, 128), F32)
PRODUCT_SCRATCH = ((128 * PRODUCT_STEP, 128), F32)


def _norm(values, gain, bias):
    center = values - jnp.mean(values, axis=0, keepdims=True)
    spread = jnp.mean(center * center, axis=0, keepdims=True)
    return (center * lax.rsqrt(spread + EPS) * gain + bias).astype(BF16)


def _column(ref, u):
    return jnp.broadcast_to(ref[u : u + 1, :], (128, 128)).T


def _project(cells, gain, bias, turned_w, turned_gate_w, scr, s):
    normed = _norm(cells.astype(F32), gain, bias)
    halves = jnp.dot(turned_w, normed, preferred_element_type=F32)
    left = jax.nn.sigmoid(halves[128:256]) * halves[:128]
    right = jax.nn.sigmoid(halves[384:]) * halves[256:384]
    scr[pl.ds(s, 128, stride=OPERAND_STEP), :] = left
    scr[pl.ds(16 + s, 128, stride=OPERAND_STEP), :] = right
    return jax.nn.sigmoid(jnp.dot(turned_gate_w, normed, preferred_element_type=F32))


def _put_operands(out_ref, scr):
    rows = scr[...].reshape(128, OPERAND_STEP, 128)[:, :32]
    out_ref[...] = rows.astype(BF16).reshape(4096, 128)


def _first_kernel(p_ref, gain_ref, bias_ref, w_ref, gw_ref, out_ref, gate_ref, turned_ref, scr):
    turned_w, turned_gate_w = w_ref[0].T, gw_ref[0].T
    gain, bias = _column(gain_ref, 0), _column(bias_ref, 0)
    for s in range(16):
        cells = jnp.concatenate([p_ref[s], p_ref[16 + s]], axis=0).T
        turned_ref[s] = cells
        gate_ref[s] = _project(cells, gain, bias, turned_w, turned_gate_w, scr, s)
    _put_operands(out_ref, scr)


def _load_products(one, two, scr):
    total = (one.astype(F32) + two.astype(F32)).reshape(128, 16, 128)
    for c in range(128):
        scr[c * PRODUCT_STEP : c * PRODUCT_STEP + 16, :] = total[c]


def _finished(scr, s, cells, gate, gain, bias, turned_w):
    mixed = _norm(scr[pl.ds(s, 128, stride=PRODUCT_STEP), :], gain, bias)
    projected = jnp.dot(turned_w, mixed, preferred_element_type=F32)
    return (cells.astype(F32) + gate * projected).astype(BF16)


def _middle_kernel(
    t_ref, p_ref, g_ref, og_ref, ob_ref, ow_ref, gain_ref, bias_ref, w_ref, gw_ref,
    mid_ref, out_ref, gate_ref, tri_scr, scr,
):
    _load_products(t_ref[:, 0], t_ref[:, 1], tri_scr)
    turned_w, turned_gate_w, turned_out_w = w_ref[1].T, gw_ref[1].T, ow_ref[0].T
    gain, bias = _column(gain_ref, 1), _column(bias_ref, 1)
    out_gain, out_bias = _column(og_ref, 0), _column(ob_ref, 0)
    for s in range(16):
        mid_ref[s] = _finished(
            tri_scr, s, p_ref[s], g_ref[s], out_gain, out_bias, turned_out_w
        )
    for s in range(16):
        gate_ref[s] = _project(mid_ref[s], gain, bias, turned_w, turned_gate_w, scr, s)
    _put_operands(out_ref, scr)


def _last_kernel(t_ref, p_ref, g_ref, og_ref, ob_ref, ow_ref, out_ref, tri_scr):
    _load_products(t_ref[0], t_ref[1], tri_scr)
    turned_w = ow_ref[1].T
    gain, bias = _column(og_ref, 1), _column(ob_ref, 1)
    for s in range(16):
        out = _finished(tri_scr, s, p_ref[s], g_ref[s], gain, bias, turned_w).T
        out_ref[s] = out[:64]
        out_ref[16 + s] = out[64:]


def _pair_up(one, two):
    low = jnp.concatenate([one[..., :64], two[..., :64]], axis=-1)
    high = jnp.concatenate([one[..., 64:], two[..., 64:]], axis=-1)
    return low, high


def _quarter(parts, q):
    return jnp.concatenate([part[..., 32 * q : 32 * q + 32] for part in parts], axis=-1)


def _put_products(out_ref, rows, tri):
    tri = tri.astype(BF16).reshape(-1, 2, 16, 1024)
    for pair in range(8):
        lanes = tri[..., pair * 128 : pair * 128 + 128]
        low, high = _pair_up(lanes[:, 0], lanes[:, 1])
        out_ref[rows, 2 * pair] = low
        out_ref[rows, 2 * pair + 1] = high


def _outgoing_kernel(core_ref, own_ref, other_ref, out_ref, l_scr, r_scr):
    core = core_ref[0]
    for pair in range(4):
        lanes = slice(pair * 128, pair * 128 + 128)
        left = _pair_up(own_ref[:, 2 * pair, 0], own_ref[:, 2 * pair + 1, 0])
        right = _pair_up(own_ref[:, 2 * pair, 1], own_ref[:, 2 * pair + 1, 1])
        away = _pair_up(other_ref[:, 2 * pair, 1], other_ref[:, 2 * pair + 1, 1])
        for b in range(2):
            l_scr[:, b, :, lanes] = left[b]
            r_scr[:, pl.ds(core, 1), b, :, lanes] = right[b][:, None]
            r_scr[:, pl.ds(1 - core, 1), b, :, lanes] = away[b][:, None]
    right = r_scr[...].reshape(1024, 512)
    for part in range(2):
        rows = slice(part * 8, part * 8 + 8)
        left = l_scr[rows].reshape(256, 512)
        tri = lax.dot_general(left, right, (((1,), (1,)), ((), ())), preferred_element_type=F32)
        _put_products(out_ref, rows, tri)


def _incoming_kernel(core_ref, own_ref, other_ref, out_ref, l_scr, r_scr):
    first = core_ref[0] == 0
    for at, ref in ((0, own_ref), (1, other_ref)):
        for zlo in range(4):
            parts = [ref[:, zlo * 4 + x, 0] for x in range(4)]
            lanes = slice(zlo * 128, zlo * 128 + 128)
            for b in range(2):
                l_scr[at, b, :, :, lanes] = jnp.where(
                    first, _quarter(parts, 2 * b), _quarter(parts, 2 * b + 1)
                )
        for pair in range(8):
            lanes = slice(pair * 128, pair * 128 + 128)
            right = _pair_up(ref[:, 2 * pair, 1], ref[:, 2 * pair + 1, 1])
            for b in range(2):
                r_scr[at, b, :, :, lanes] = right[b]
    right = r_scr[...].reshape(512, 1024)
    for part in range(2):
        left = l_scr[:, :, :, :, part * 256 : part * 256 + 256].reshape(512, 256)
        tri = lax.dot_general(left, right, (((0,), (0,)), ((), ())), preferred_element_type=F32)
        _put_products(out_ref, slice(part * 8, part * 8 + 8), tri)


def _call(kernel, outs, scratch, args, scalar=False, fetch=False):
    whole = pl.BlockSpec(memory_space=pltpu.VMEM)
    specs = [whole for _ in args]
    grid = ()
    if scalar:
        specs[0] = pl.BlockSpec(memory_space=pltpu.SMEM)
    if fetch:
        grid = (1,)
        specs = [pl.BlockSpec(arg.shape, lambda i, n=arg.ndim: (0,) * n) for arg in args]
    return pl.pallas_call(
        kernel,
        grid=grid,
        out_shape=[jax.ShapeDtypeStruct(shape, dtype) for shape, dtype in outs],
        in_specs=specs,
        out_specs=[whole for _ in outs],
        scratch_shapes=[pltpu.VMEM(shape, dtype) for shape, dtype in scratch],
        compiler_params=pltpu.CompilerParams(vmem_limit_bytes=(60 if fetch else 40) << 20),
    )(*args)


def _exchange(tiles, group):
    return lax.all_to_all(tiles, group, split_axis=0, concat_axis=0, tiled=True)


def _products(kernel, group, sources, scratch, tiles):
    own = _exchange(tiles.reshape(128, 32, 128), group).reshape(*sources, 2, 16, 128)
    other = lax.ppermute(own, "core", [(0, 1), (1, 0)])
    core = lax.axis_index("core").astype(jnp.int32).reshape(1)
    (out,) = _call(
        kernel, [((16, 16, 16, 128), BF16)], scratch, (core, own, other), scalar=True
    )
    return _exchange(out.reshape(256, 16, 128), ("zhi", "y", "zlo", "xhi", "xlo"))


def body(pair_rep, in_gain, in_bias, proj_w, gate_w, out_gain, out_bias, out_w):
    turned = (16, 128, 128)
    tiles, gate, cells = _call(
        _first_kernel,
        [((4096, 128), BF16), (turned, F32), (turned, BF16)],
        [OPERAND_SCRATCH],
        (pair_rep, in_gain, in_bias, proj_w, gate_w),
        fetch=True,
    )
    tri = _products(
        _outgoing_kernel,
        OUTGOING,
        (16, 8),
        [((16, 2, 16, 512), BF16), ((16, 2, 2, 16, 512), BF16)],
        tiles,
    ).reshape(64, 2, 2, 16, 128)
    middle, tiles, gate = _call(
        _middle_kernel,
        [(turned, BF16), ((4096, 128), BF16), (turned, F32)],
        [PRODUCT_SCRATCH, OPERAND_SCRATCH],
        (tri, cells, gate, out_gain, out_bias, out_w, in_gain, in_bias, proj_w, gate_w),
    )
    tri = _products(
        _incoming_kernel,
        INCOMING,
        (8, 16),
        [((2, 2, 8, 16, 512), BF16), ((2, 2, 8, 16, 1024), BF16)],
        tiles,
    ).reshape(2, 128, 16, 128)
    (out,) = _call(
        _last_kernel,
        [(pair_rep.shape, BF16)],
        [PRODUCT_SCRATCH],
        (tri, middle, gate, out_gain, out_bias, out_w),
    )
    return out


def solution(mesh):
    fine = Mesh(
        mesh.devices.reshape(2, 8, 2, 4, 2, 2), ("zhi", "y", "core", "zlo", "xhi", "xlo")
    )
    cells = P(("zhi", "y", "core"), ("zlo", "xhi", "xlo"), None)
    placed = (cells, P(), P(), P(), P(), P(), P(), P())
    return jax.shard_map(body, mesh=fine, in_specs=placed, out_specs=cells, check_vma=False)
```

```python
import functools

import jax
import jax.numpy as jnp
from jax import lax
from jax.experimental import pallas as pl
from jax.experimental.pallas import tpu as pltpu
from jax.sharding import Mesh
from jax.sharding import PartitionSpec as P

OUTGOING = ("zhi", "yhi", "ylo", "zlo", "xlo")
INCOMING = ("zhi", "ylo", "zlo", "xhi", "xlo")
EPS = 1e-05
F32 = jnp.float32
BF16 = jnp.bfloat16

OPERAND_STEP = 40
PRODUCT_STEP = 24
STEP_ROWS = 16
OPERAND_SCRATCH = ((128 * OPERAND_STEP, 128), F32)
PRODUCT_SCRATCH = ((128 * PRODUCT_STEP, 128), F32)


def _norm(values, gain, bias):
    center = values - jnp.mean(values, axis=0, keepdims=True)
    spread = jnp.mean(center * center, axis=0, keepdims=True)
    return (center * lax.rsqrt(spread + EPS) * gain + bias).astype(BF16)


def _column(row):
    return jnp.broadcast_to(row, (128, 128)).T


def _project(cells, gain, bias, turned_w, turned_gate_w, scr, s):
    normed = _norm(cells.astype(F32), gain, bias)
    halves = jnp.dot(turned_w, normed, preferred_element_type=F32)
    left = jax.nn.sigmoid(halves[128:256]) * halves[:128]
    right = jax.nn.sigmoid(halves[384:]) * halves[256:384]
    scr[pl.ds(s, 128, stride=OPERAND_STEP), :] = left
    scr[pl.ds(16 + s, 128, stride=OPERAND_STEP), :] = right
    return jax.nn.sigmoid(jnp.dot(turned_gate_w, normed, preferred_element_type=F32))


def _put_operands(out_ref, scr):
    rows = scr[...].reshape(128, OPERAND_STEP, 128)[:, :32]
    out_ref[...] = rows.astype(BF16).reshape(4096, 128)


def _first_kernel(
    p_ref, gain_ref, bias_ref, w_ref, gw_ref, og_ref, ob_ref,
    out_ref, gate_ref, turned_ref, columns_ref, scr,
):
    step = pl.program_id(0)
    turned_w, turned_gate_w = w_ref[0].T, gw_ref[0].T
    gain, bias = _column(gain_ref[:1]), _column(bias_ref[:1])
    for at in range(STEP_ROWS):
        cells = jnp.concatenate([p_ref[0, at], p_ref[1, at]], axis=0).T
        turned_ref[at] = cells
        s = step * STEP_ROWS + at
        gate_ref[at] = _project(cells, gain, bias, turned_w, turned_gate_w, scr, s)

    @pl.when(step == pl.num_programs(0) - 1)
    def _():
        _put_operands(out_ref, scr)
        columns_ref[0] = _column(gain_ref[1:])
        columns_ref[1] = _column(bias_ref[1:])
        for u in range(2):
            columns_ref[2 + 2 * u] = _column(og_ref[u : u + 1])
            columns_ref[3 + 2 * u] = _column(ob_ref[u : u + 1])


def _load_products(one, two, scr):
    total = (one.astype(F32) + two.astype(F32)).reshape(128, 16, 128)
    for c in range(128):
        scr[c * PRODUCT_STEP : c * PRODUCT_STEP + 16, :] = total[c]


def _finished(scr, s, cells, gate, gain, bias, turned_w):
    mixed = _norm(scr[pl.ds(s, 128, stride=PRODUCT_STEP), :], gain, bias)
    projected = jnp.dot(turned_w, mixed, preferred_element_type=F32)
    return (cells.astype(F32) + gate * projected).astype(BF16)


def _middle_kernel(
    t_ref, p_ref, g_ref, columns_ref, ow_ref, w_ref, gw_ref,
    mid_ref, out_ref, gate_ref, tri_scr, scr,
):
    _load_products(t_ref[:, 0], t_ref[:, 1], tri_scr)
    turned_w, turned_gate_w, turned_out_w = w_ref[1].T, gw_ref[1].T, ow_ref[0].T
    gain, bias = columns_ref[0], columns_ref[1]
    out_gain, out_bias = columns_ref[2], columns_ref[3]
    for s in range(16):
        mid_ref[s] = _finished(
            tri_scr, s, p_ref[s], g_ref[s], out_gain, out_bias, turned_out_w
        )
    for s in range(16):
        gate_ref[s] = _project(mid_ref[s], gain, bias, turned_w, turned_gate_w, scr, s)
    _put_operands(out_ref, scr)


def _last_kernel(t_ref, p_ref, g_ref, columns_ref, ow_ref, out_ref, tri_scr):
    _load_products(t_ref[:, 0], t_ref[:, 1], tri_scr)
    turned_w = ow_ref[1].T
    gain, bias = columns_ref[4], columns_ref[5]
    for s in range(16):
        out = _finished(tri_scr, s, p_ref[s], g_ref[s], gain, bias, turned_w).T
        out_ref[s] = out[:64]
        out_ref[16 + s] = out[64:]


def _pair_up(one, two):
    low = jnp.concatenate([one[..., :64], two[..., :64]], axis=-1)
    high = jnp.concatenate([one[..., 64:], two[..., 64:]], axis=-1)
    return low, high


def _quarter(parts, q):
    return jnp.concatenate([part[..., 32 * q : 32 * q + 32] for part in parts], axis=-1)


def _put_products(out_ref, rows, tri):
    tri = tri.astype(BF16).reshape(-1, 2, 16, 1024)
    for pair in range(8):
        lanes = tri[..., pair * 128 : pair * 128 + 128]
        low, high = _pair_up(lanes[:, 0], lanes[:, 1])
        out_ref[rows, 2 * pair] = low
        out_ref[rows, 2 * pair + 1] = high


def _outgoing_kernel(core_ref, own_ref, other_ref, out_ref, l_scr, r_scr):
    core = core_ref[0]
    for pair in range(4):
        lanes = slice(pair * 128, pair * 128 + 128)
        left = _pair_up(own_ref[:, 2 * pair, 0], own_ref[:, 2 * pair + 1, 0])
        right = _pair_up(own_ref[:, 2 * pair, 1], own_ref[:, 2 * pair + 1, 1])
        away = _pair_up(other_ref[:, 2 * pair, 1], other_ref[:, 2 * pair + 1, 1])
        for b in range(2):
            l_scr[:, b, :, lanes] = left[b]
            r_scr[:, pl.ds(core, 1), b, :, lanes] = right[b][:, None]
            r_scr[:, pl.ds(1 - core, 1), b, :, lanes] = away[b][:, None]
    right = r_scr[...].reshape(1024, 512)
    for part in range(2):
        rows = slice(part * 8, part * 8 + 8)
        left = l_scr[rows].reshape(256, 512)
        tri = lax.dot_general(left, right, (((1,), (1,)), ((), ())), preferred_element_type=F32)
        _put_products(out_ref, rows, tri)


def _incoming_kernel(core_ref, own_ref, other_ref, out_ref, l_scr, r_scr):
    def load_left(core):
        for at, ref in ((0, own_ref), (1, other_ref)):
            for zlo in range(4):
                parts = [ref[:, zlo * 4 + x, 0] for x in range(4)]
                lanes = slice(zlo * 128, zlo * 128 + 128)
                for b in range(2):
                    l_scr[at, b, :, :, lanes] = _quarter(parts, 2 * b + core)

    for core in range(2):
        pl.when(core_ref[0] == core)(functools.partial(load_left, core))
    for at, ref in ((0, own_ref), (1, other_ref)):
        for pair in range(8):
            lanes = slice(pair * 128, pair * 128 + 128)
            right = _pair_up(ref[:, 2 * pair, 1], ref[:, 2 * pair + 1, 1])
            for b in range(2):
                r_scr[at, b, :, :, lanes] = right[b]
    right = r_scr[...].reshape(512, 1024)
    for part in range(2):
        left = l_scr[:, :, :, :, part * 256 : part * 256 + 256].reshape(512, 256)
        tri = lax.dot_general(left, right, (((0,), (0,)), ((), ())), preferred_element_type=F32)
        _put_products(out_ref, slice(part * 8, part * 8 + 8), tri)


def _call(kernel, outs, scratch, args, scalar=False):
    whole = pl.BlockSpec(memory_space=pltpu.VMEM)
    specs = [whole for _ in args]
    if scalar:
        specs[0] = pl.BlockSpec(memory_space=pltpu.SMEM)
    return pl.pallas_call(
        kernel,
        out_shape=[jax.ShapeDtypeStruct(shape, dtype) for shape, dtype in outs],
        in_specs=specs,
        out_specs=[whole for _ in outs],
        scratch_shapes=[pltpu.VMEM(shape, dtype) for shape, dtype in scratch],
        compiler_params=pltpu.CompilerParams(vmem_limit_bytes=40 << 20),
    )(*args)


def _first(pair_rep, *params):
    def whole(shape):
        return pl.BlockSpec(shape, lambda i: (0,) * len(shape))

    def part(shape, at):
        return pl.BlockSpec(shape, lambda i: tuple(i if d == at else 0 for d in range(len(shape))))

    return pl.pallas_call(
        _first_kernel,
        grid=(16 // STEP_ROWS,),
        out_shape=[
            jax.ShapeDtypeStruct((4096, 128), BF16),
            jax.ShapeDtypeStruct((16, 128, 128), F32),
            jax.ShapeDtypeStruct((16, 128, 128), BF16),
            jax.ShapeDtypeStruct((6, 128, 128), F32),
        ],
        in_specs=[part((2, STEP_ROWS, 64, 128), 1)] + [whole(arg.shape) for arg in params],
        out_specs=[
            whole((4096, 128)),
            part((STEP_ROWS, 128, 128), 0),
            part((STEP_ROWS, 128, 128), 0),
            whole((6, 128, 128)),
        ],
        scratch_shapes=[pltpu.VMEM(*OPERAND_SCRATCH)],
        compiler_params=pltpu.CompilerParams(vmem_limit_bytes=60 << 20),
    )(pair_rep.reshape(2, 16, 64, 128), *params)


def _exchange(tiles, group):
    return lax.all_to_all(tiles, group, split_axis=0, concat_axis=0, tiled=True)


def _products(kernel, group, sources, scratch, tiles):
    own = _exchange(tiles.reshape(128, 32, 128), group).reshape(*sources, 2, 16, 128)
    other = lax.ppermute(own, "core", [(0, 1), (1, 0)])
    core = lax.axis_index("core").astype(jnp.int32).reshape(1)
    (out,) = _call(
        kernel, [((16, 16, 16, 128), BF16)], scratch, (core, own, other), scalar=True
    )
    return _exchange(out.reshape(256, 16, 128), ("zhi", "yhi", "ylo", "zlo", "xhi", "xlo"))


def body(pair_rep, in_gain, in_bias, proj_w, gate_w, out_gain, out_bias, out_w):
    turned = (16, 128, 128)
    tiles, gate, cells, columns = _first(
        pair_rep, in_gain, in_bias, proj_w, gate_w, out_gain, out_bias
    )
    tri = _products(
        _outgoing_kernel,
        OUTGOING,
        (16, 8),
        [((16, 2, 16, 512), BF16), ((16, 2, 2, 16, 512), BF16)],
        tiles,
    ).reshape(64, 2, 2, 16, 128)
    middle, tiles, gate = _call(
        _middle_kernel,
        [(turned, BF16), ((4096, 128), BF16), (turned, F32)],
        [PRODUCT_SCRATCH, OPERAND_SCRATCH],
        (tri, cells, gate, columns, out_w, proj_w, gate_w),
    )
    tri = _products(
        _incoming_kernel,
        INCOMING,
        (8, 16),
        [((2, 2, 8, 16, 512), BF16), ((2, 2, 8, 16, 1024), BF16)],
        tiles,
    ).reshape(2, 2, 64, 16, 128)
    (out,) = _call(
        _last_kernel,
        [(pair_rep.shape, BF16)],
        [PRODUCT_SCRATCH],
        (tri, middle, gate, columns, out_w),
    )
    return out


def solution(mesh):
    fine = Mesh(
        mesh.devices.reshape(2, 2, 4, 2, 4, 2, 2),
        ("zhi", "yhi", "ylo", "core", "zlo", "xhi", "xlo"),
    )
    cells = P(("zhi", "yhi", "ylo", "core"), ("zlo", "xhi", "xlo"), None)
    placed = (cells, P(), P(), P(), P(), P(), P(), P())
    return jax.shard_map(body, mesh=fine, in_specs=placed, out_specs=cells, check_vma=False)
```

```python
import functools

import jax
import jax.numpy as jnp
from jax import lax
from jax.experimental import pallas as pl
from jax.experimental.pallas import tpu as pltpu
from jax.sharding import Mesh
from jax.sharding import PartitionSpec as P

OUTGOING = ("zhi", "yhi", "ylo", "zlo", "xlo")
INCOMING = ("zhi", "ylo", "zlo", "xhi", "xlo")
EPS = 1e-05
F32 = jnp.float32
BF16 = jnp.bfloat16

OPERAND_STEP = 40
PRODUCT_STEP = 24
OPERAND_SCRATCH = ((129 * OPERAND_STEP, 128), F32)
PRODUCT_SCRATCH = ((129 * PRODUCT_STEP, 128), F32)


def _norm(values, gain, bias):
    center = values - jnp.mean(values, axis=0, keepdims=True)
    spread = jnp.mean(center * center, axis=0, keepdims=True)
    return (center * lax.rsqrt(spread + EPS) * gain + bias).astype(BF16)


def _column(row):
    return jnp.broadcast_to(row, (128, 128)).T


def _beside(one, two):
    return jnp.concatenate([one, two], axis=1)


def _twice(one):
    return _beside(one, one)


def _put_two(ref, s, value):
    ref[s] = value[:, :128]
    ref[s + 1] = value[:, 128:]


def _project(cells, gain, bias, turned_w, turned_gate_w, scr, s):
    normed = _norm(cells.astype(F32), gain, bias)
    halves = jnp.dot(turned_w, normed, preferred_element_type=F32)
    left = jax.nn.sigmoid(halves[128:256]) * halves[:128]
    right = jax.nn.sigmoid(halves[384:]) * halves[256:384]
    for i in range(2):
        lanes = slice(128 * i, 128 * i + 128)
        scr[pl.ds(s + i, 128, stride=OPERAND_STEP), :] = left[:, lanes]
        scr[pl.ds(16 + s + i, 128, stride=OPERAND_STEP), :] = right[:, lanes]
    return jax.nn.sigmoid(jnp.dot(turned_gate_w, normed, preferred_element_type=F32))


def _put_operands(out_ref, scr):
    rows = scr[: 128 * OPERAND_STEP].reshape(128, OPERAND_STEP, 128)[:, :32]
    out_ref[...] = rows.astype(BF16).reshape(4096, 128)


def _first_kernel(
    p_ref, gain_ref, bias_ref, w_ref, gw_ref, og_ref, ob_ref,
    out_ref, gate_ref, turned_ref, columns_ref, scr,
):
    turned_w, turned_gate_w = w_ref[0].T, gw_ref[0].T
    gain, bias = _twice(_column(gain_ref[:1])), _twice(_column(bias_ref[:1]))
    for s in range(0, 16, 2):
        one = jnp.concatenate([p_ref[s], p_ref[16 + s]], axis=0).T
        two = jnp.concatenate([p_ref[s + 1], p_ref[17 + s]], axis=0).T
        turned_ref[s] = one
        turned_ref[s + 1] = two
        cells = _beside(one, two)
        gate = _project(cells, gain, bias, turned_w, turned_gate_w, scr, s)
        _put_two(gate_ref, s, gate)
    _put_operands(out_ref, scr)
    columns_ref[0] = _column(gain_ref[1:])
    columns_ref[1] = _column(bias_ref[1:])
    for u in range(2):
        columns_ref[2 + 2 * u] = _column(og_ref[u : u + 1])
        columns_ref[3 + 2 * u] = _column(ob_ref[u : u + 1])


def _load_products(one, two, scr):
    total = (one.astype(F32) + two.astype(F32)).reshape(128, 16, 128)
    for c in range(128):
        scr[c * PRODUCT_STEP : c * PRODUCT_STEP + 16, :] = total[c]


def _finished(scr, s, p_ref, g_ref, gain, bias, turned_w):
    tri = _beside(
        scr[pl.ds(s, 128, stride=PRODUCT_STEP), :], scr[pl.ds(s + 1, 128, stride=PRODUCT_STEP), :]
    )
    mixed = _norm(tri, gain, bias)
    projected = jnp.dot(turned_w, mixed, preferred_element_type=F32)
    cells = _beside(p_ref[s], p_ref[s + 1]).astype(F32)
    return (cells + _beside(g_ref[s], g_ref[s + 1]) * projected).astype(BF16)


def _middle_kernel(
    t_ref, p_ref, g_ref, columns_ref, ow_ref, w_ref, gw_ref,
    mid_ref, out_ref, gate_ref, tri_scr, scr,
):
    _load_products(t_ref[:, 0], t_ref[:, 1], tri_scr)
    turned_w, turned_gate_w, turned_out_w = w_ref[1].T, gw_ref[1].T, ow_ref[0].T
    gain, bias, out_gain, out_bias = (_twice(columns_ref[i]) for i in range(4))
    for s in range(0, 16, 2):
        mid = _finished(tri_scr, s, p_ref, g_ref, out_gain, out_bias, turned_out_w)
        _put_two(mid_ref, s, mid)
    for s in range(0, 16, 2):
        cells = _beside(mid_ref[s], mid_ref[s + 1])
        gate = _project(cells, gain, bias, turned_w, turned_gate_w, scr, s)
        _put_two(gate_ref, s, gate)
    _put_operands(out_ref, scr)


def _last_kernel(t_ref, p_ref, g_ref, columns_ref, ow_ref, out_ref, tri_scr):
    _load_products(t_ref[:, 0], t_ref[:, 1], tri_scr)
    turned_w = ow_ref[1].T
    gain, bias = _twice(columns_ref[4]), _twice(columns_ref[5])
    for s in range(0, 16, 2):
        out = _finished(tri_scr, s, p_ref, g_ref, gain, bias, turned_w).T
        out_ref[s] = out[:64]
        out_ref[16 + s] = out[64:128]
        out_ref[s + 1] = out[128:192]
        out_ref[17 + s] = out[192:]


def _pair_up(one, two):
    low = jnp.concatenate([one[..., :64], two[..., :64]], axis=-1)
    high = jnp.concatenate([one[..., 64:], two[..., 64:]], axis=-1)
    return low, high


def _quarter(parts, q):
    return jnp.concatenate([part[..., 32 * q : 32 * q + 32] for part in parts], axis=-1)


def _put_products(out_ref, rows, tri):
    tri = tri.astype(BF16).reshape(-1, 2, 16, 1024)
    for pair in range(8):
        lanes = tri[..., pair * 128 : pair * 128 + 128]
        low, high = _pair_up(lanes[:, 0], lanes[:, 1])
        out_ref[rows, 2 * pair] = low
        out_ref[rows, 2 * pair + 1] = high


def _outgoing_kernel(core_ref, own_ref, other_ref, out_ref, l_scr, r_scr):
    core = core_ref[0]
    for pair in range(4):
        lanes = slice(pair * 128, pair * 128 + 128)
        left = _pair_up(own_ref[:, 2 * pair, 0], own_ref[:, 2 * pair + 1, 0])
        right = _pair_up(own_ref[:, 2 * pair, 1], own_ref[:, 2 * pair + 1, 1])
        away = _pair_up(other_ref[:, 2 * pair, 1], other_ref[:, 2 * pair + 1, 1])
        for b in range(2):
            l_scr[:, b, :, lanes] = left[b]
            r_scr[:, pl.ds(core, 1), b, :, lanes] = right[b][:, None]
            r_scr[:, pl.ds(1 - core, 1), b, :, lanes] = away[b][:, None]
    right = r_scr[...].reshape(1024, 512)
    for part in range(2):
        rows = slice(part * 8, part * 8 + 8)
        left = l_scr[rows].reshape(256, 512)
        tri = lax.dot_general(left, right, (((1,), (1,)), ((), ())), preferred_element_type=F32)
        _put_products(out_ref, rows, tri)


def _incoming_kernel(core_ref, own_ref, other_ref, out_ref, l_scr, r_scr):
    def load_left(core):
        for at, ref in ((0, own_ref), (1, other_ref)):
            for zlo in range(4):
                parts = [ref[:, zlo * 4 + x, 0] for x in range(4)]
                lanes = slice(zlo * 128, zlo * 128 + 128)
                for b in range(2):
                    l_scr[at, b, :, :, lanes] = _quarter(parts, 2 * b + core)

    for core in range(2):
        pl.when(core_ref[0] == core)(functools.partial(load_left, core))
    for at, ref in ((0, own_ref), (1, other_ref)):
        for pair in range(8):
            lanes = slice(pair * 128, pair * 128 + 128)
            right = _pair_up(ref[:, 2 * pair, 1], ref[:, 2 * pair + 1, 1])
            for b in range(2):
                r_scr[at, b, :, :, lanes] = right[b]
    right = r_scr[...].reshape(512, 1024)
    for part in range(2):
        left = l_scr[:, :, :, :, part * 256 : part * 256 + 256].reshape(512, 256)
        tri = lax.dot_general(left, right, (((0,), (0,)), ((), ())), preferred_element_type=F32)
        _put_products(out_ref, slice(part * 8, part * 8 + 8), tri)


def _call(kernel, outs, scratch, args, scalar=False):
    whole = pl.BlockSpec(memory_space=pltpu.VMEM)
    specs = [whole for _ in args]
    if scalar:
        specs[0] = pl.BlockSpec(memory_space=pltpu.SMEM)
    return pl.pallas_call(
        kernel,
        out_shape=[jax.ShapeDtypeStruct(shape, dtype) for shape, dtype in outs],
        in_specs=specs,
        out_specs=[whole for _ in outs],
        scratch_shapes=[pltpu.VMEM(shape, dtype) for shape, dtype in scratch],
        compiler_params=pltpu.CompilerParams(vmem_limit_bytes=40 << 20),
    )(*args)


def _first(*args):
    def whole(shape):
        return pl.BlockSpec(shape, lambda i: (0,) * len(shape))

    in_specs = [whole(arg.shape) for arg in args]
    in_specs[3] = pl.BlockSpec((1, 128, 512), lambda i: (0, 0, 0))
    in_specs[4] = pl.BlockSpec((1, 128, 128), lambda i: (0, 0, 0))
    outs = [((4096, 128), BF16), ((16, 128, 128), F32), ((16, 128, 128), BF16), ((6, 128, 128), F32)]
    return pl.pallas_call(
        _first_kernel,
        grid=(1,),
        out_shape=[jax.ShapeDtypeStruct(shape, dtype) for shape, dtype in outs],
        in_specs=in_specs,
        out_specs=[whole(shape) for shape, _ in outs],
        scratch_shapes=[pltpu.VMEM(*OPERAND_SCRATCH)],
        compiler_params=pltpu.CompilerParams(vmem_limit_bytes=60 << 20),
    )(*args)


def _exchange(tiles, group):
    return lax.all_to_all(tiles, group, split_axis=0, concat_axis=0, tiled=True)


def _products(kernel, group, sources, scratch, tiles):
    own = _exchange(tiles.reshape(128, 32, 128), group).reshape(*sources, 2, 16, 128)
    other = lax.ppermute(own, "core", [(0, 1), (1, 0)])
    core = lax.axis_index("core").astype(jnp.int32).reshape(1)
    (out,) = _call(
        kernel, [((16, 16, 16, 128), BF16)], scratch, (core, own, other), scalar=True
    )
    return _exchange(out.reshape(256, 16, 128), ("zhi", "yhi", "ylo", "zlo", "xhi", "xlo"))


def body(pair_rep, in_gain, in_bias, proj_w, gate_w, out_gain, out_bias, out_w):
    turned = (16, 128, 128)
    tiles, gate, cells, columns = _first(
        pair_rep, in_gain, in_bias, proj_w, gate_w, out_gain, out_bias
    )
    tri = _products(
        _outgoing_kernel,
        OUTGOING,
        (16, 8),
        [((16, 2, 16, 512), BF16), ((16, 2, 2, 16, 512), BF16)],
        tiles,
    ).reshape(64, 2, 2, 16, 128)
    middle, tiles, gate = _call(
        _middle_kernel,
        [(turned, BF16), ((4096, 128), BF16), (turned, F32)],
        [PRODUCT_SCRATCH, OPERAND_SCRATCH],
        (tri, cells, gate, columns, out_w, proj_w, gate_w),
    )
    tri = _products(
        _incoming_kernel,
        INCOMING,
        (8, 16),
        [((2, 2, 8, 16, 512), BF16), ((2, 2, 8, 16, 1024), BF16)],
        tiles,
    ).reshape(2, 2, 64, 16, 128)
    (out,) = _call(
        _last_kernel,
        [(pair_rep.shape, BF16)],
        [PRODUCT_SCRATCH],
        (tri, middle, gate, columns, out_w),
    )
    return out


def solution(mesh):
    fine = Mesh(
        mesh.devices.reshape(2, 2, 4, 2, 4, 2, 2),
        ("zhi", "yhi", "ylo", "core", "zlo", "xhi", "xlo"),
    )
    cells = P(("zhi", "yhi", "ylo", "core"), ("zlo", "xhi", "xlo"), None)
    placed = (cells, P(), P(), P(), P(), P(), P(), P())
    return jax.shard_map(body, mesh=fine, in_specs=placed, out_specs=cells, check_vma=False)
```

```python
import functools

import jax
import jax.numpy as jnp
from jax import lax
from jax.experimental import pallas as pl
from jax.experimental.pallas import tpu as pltpu
from jax.sharding import Mesh
from jax.sharding import PartitionSpec as P

OUTGOING = ("zhi", "yhi", "ylo", "zlo", "xlo")
INCOMING = ("zhi", "ylo", "zlo", "xhi", "xlo")
EPS = 1e-05
F32 = jnp.float32
BF16 = jnp.bfloat16

OPERAND_STEP = 40
PRODUCT_STEP = 24
OPERAND_SCRATCH = ((129 * OPERAND_STEP, 128), F32)
PRODUCT_SCRATCH = ((129 * PRODUCT_STEP, 128), F32)


def _norm(values, gain, bias):
    center = values - jnp.mean(values, axis=0, keepdims=True)
    spread = jnp.mean(center * center, axis=0, keepdims=True)
    return (center * lax.rsqrt(spread + EPS) * gain + bias).astype(BF16)


def _column(row):
    return jnp.broadcast_to(row, (128, 128)).T


def _beside(one, two):
    return jnp.concatenate([one, two], axis=1)


def _twice(one):
    return _beside(one, one)


def _put_two(ref, s, value):
    ref[s] = value[:, :128]
    ref[s + 1] = value[:, 128:]


def _project(cells, gain, bias, turned_w, scr, s):
    normed = _norm(cells.astype(F32), gain, bias)
    halves = jnp.dot(turned_w, normed, preferred_element_type=F32)
    left = jax.nn.sigmoid(halves[128:256]) * halves[:128]
    right = jax.nn.sigmoid(halves[384:]) * halves[256:384]
    for i in range(2):
        lanes = slice(128 * i, 128 * i + 128)
        scr[pl.ds(s + i, 128, stride=OPERAND_STEP), :] = left[:, lanes]
        scr[pl.ds(16 + s + i, 128, stride=OPERAND_STEP), :] = right[:, lanes]


def _gate(cells, gain, bias, turned_gate_w):
    normed = _norm(cells.astype(F32), gain, bias)
    return jax.nn.sigmoid(jnp.dot(turned_gate_w, normed, preferred_element_type=F32))


def _put_operands(out_ref, scr):
    rows = scr[: 128 * OPERAND_STEP].reshape(128, OPERAND_STEP, 128)[:, :32]
    out_ref[...] = rows.astype(BF16).reshape(4096, 128)


def _turned_rows(p_ref, s):
    return jnp.concatenate([p_ref[s], p_ref[16 + s]], axis=0).T


def _first_kernel(p_ref, gain_ref, bias_ref, w_ref, out_ref, scr):
    turned_w = w_ref[0].T
    gain, bias = _twice(_column(gain_ref[:1])), _twice(_column(bias_ref[:1]))
    for s in range(0, 16, 2):
        cells = _beside(_turned_rows(p_ref, s), _turned_rows(p_ref, s + 1))
        _project(cells, gain, bias, turned_w, scr, s)
    _put_operands(out_ref, scr)


def _first_gate_kernel(
    p_ref, gain_ref, bias_ref, gw_ref, og_ref, ob_ref, gate_ref, turned_ref, columns_ref
):
    turned_gate_w = gw_ref[0].T
    gain, bias = _twice(_column(gain_ref[:1])), _twice(_column(bias_ref[:1]))
    for s in range(0, 16, 2):
        cells = _beside(_turned_rows(p_ref, s), _turned_rows(p_ref, s + 1))
        _put_two(turned_ref, s, cells)
        _put_two(gate_ref, s, _gate(cells, gain, bias, turned_gate_w))
    columns_ref[0] = _column(gain_ref[1:])
    columns_ref[1] = _column(bias_ref[1:])
    for u in range(2):
        columns_ref[2 + 2 * u] = _column(og_ref[u : u + 1])
        columns_ref[3 + 2 * u] = _column(ob_ref[u : u + 1])


def _middle_gate_kernel(p_ref, columns_ref, gw_ref, gate_ref):
    turned_gate_w = gw_ref[1].T
    gain, bias = (_twice(columns_ref[i]) for i in range(2))
    for s in range(0, 16, 2):
        cells = _beside(p_ref[s], p_ref[s + 1])
        _put_two(gate_ref, s, _gate(cells, gain, bias, turned_gate_w))


def _load_products(one, two, scr):
    total = (one.astype(F32) + two.astype(F32)).reshape(128, 16, 128)
    for c in range(128):
        scr[c * PRODUCT_STEP : c * PRODUCT_STEP + 16, :] = total[c]


def _finished(scr, s, p_ref, g_ref, gain, bias, turned_w):
    tri = _beside(
        scr[pl.ds(s, 128, stride=PRODUCT_STEP), :], scr[pl.ds(s + 1, 128, stride=PRODUCT_STEP), :]
    )
    mixed = _norm(tri, gain, bias)
    projected = jnp.dot(turned_w, mixed, preferred_element_type=F32)
    cells = _beside(p_ref[s], p_ref[s + 1]).astype(F32)
    return (cells + _beside(g_ref[s], g_ref[s + 1]) * projected).astype(BF16)


def _middle_kernel(
    t_ref, p_ref, g_ref, columns_ref, ow_ref, w_ref, mid_ref, out_ref, tri_scr, scr
):
    _load_products(t_ref[:, 0], t_ref[:, 1], tri_scr)
    turned_w, turned_out_w = w_ref[1].T, ow_ref[0].T
    gain, bias, out_gain, out_bias = (_twice(columns_ref[i]) for i in range(4))
    for s in range(0, 16, 2):
        mid = _finished(tri_scr, s, p_ref, g_ref, out_gain, out_bias, turned_out_w)
        _put_two(mid_ref, s, mid)
    for s in range(0, 16, 2):
        _project(_beside(mid_ref[s], mid_ref[s + 1]), gain, bias, turned_w, scr, s)
    _put_operands(out_ref, scr)


def _last_kernel(t_ref, p_ref, g_ref, columns_ref, ow_ref, out_ref, tri_scr):
    _load_products(t_ref[:, 0], t_ref[:, 1], tri_scr)
    turned_w = ow_ref[1].T
    gain, bias = _twice(columns_ref[4]), _twice(columns_ref[5])
    for s in range(0, 16, 2):
        out = _finished(tri_scr, s, p_ref, g_ref, gain, bias, turned_w).T
        out_ref[s] = out[:64]
        out_ref[16 + s] = out[64:128]
        out_ref[s + 1] = out[128:192]
        out_ref[17 + s] = out[192:]


def _pair_up(one, two):
    low = jnp.concatenate([one[..., :64], two[..., :64]], axis=-1)
    high = jnp.concatenate([one[..., 64:], two[..., 64:]], axis=-1)
    return low, high


def _quarter(parts, q):
    return jnp.concatenate([part[..., 32 * q : 32 * q + 32] for part in parts], axis=-1)


def _put_products(out_ref, rows, tri):
    tri = tri.astype(BF16).reshape(-1, 2, 16, 1024)
    for pair in range(8):
        lanes = tri[..., pair * 128 : pair * 128 + 128]
        low, high = _pair_up(lanes[:, 0], lanes[:, 1])
        out_ref[rows, 2 * pair] = low
        out_ref[rows, 2 * pair + 1] = high


def _outgoing_kernel(core_ref, own_ref, other_ref, out_ref, l_scr, r_scr):
    core = core_ref[0]
    for pair in range(4):
        lanes = slice(pair * 128, pair * 128 + 128)
        left = _pair_up(own_ref[:, 2 * pair, 0], own_ref[:, 2 * pair + 1, 0])
        right = _pair_up(own_ref[:, 2 * pair, 1], own_ref[:, 2 * pair + 1, 1])
        away = _pair_up(other_ref[:, 2 * pair, 1], other_ref[:, 2 * pair + 1, 1])
        for b in range(2):
            l_scr[:, b, :, lanes] = left[b]
            r_scr[:, pl.ds(core, 1), b, :, lanes] = right[b][:, None]
            r_scr[:, pl.ds(1 - core, 1), b, :, lanes] = away[b][:, None]
    right = r_scr[...].reshape(1024, 512)
    for part in range(2):
        rows = slice(part * 8, part * 8 + 8)
        left = l_scr[rows].reshape(256, 512)
        tri = lax.dot_general(left, right, (((1,), (1,)), ((), ())), preferred_element_type=F32)
        _put_products(out_ref, rows, tri)


def _incoming_kernel(core_ref, own_ref, other_ref, out_ref, l_scr, r_scr):
    def load_left(core):
        for at, ref in ((0, own_ref), (1, other_ref)):
            for zlo in range(4):
                parts = [ref[:, zlo * 4 + x, 0] for x in range(4)]
                lanes = slice(zlo * 128, zlo * 128 + 128)
                for b in range(2):
                    l_scr[at, b, :, :, lanes] = _quarter(parts, 2 * b + core)

    for core in range(2):
        pl.when(core_ref[0] == core)(functools.partial(load_left, core))
    for at, ref in ((0, own_ref), (1, other_ref)):
        for pair in range(8):
            lanes = slice(pair * 128, pair * 128 + 128)
            right = _pair_up(ref[:, 2 * pair, 1], ref[:, 2 * pair + 1, 1])
            for b in range(2):
                r_scr[at, b, :, :, lanes] = right[b]
    right = r_scr[...].reshape(512, 1024)
    for part in range(2):
        left = l_scr[:, :, :, :, part * 256 : part * 256 + 256].reshape(512, 256)
        tri = lax.dot_general(left, right, (((0,), (0,)), ((), ())), preferred_element_type=F32)
        _put_products(out_ref, slice(part * 8, part * 8 + 8), tri)


def _call(kernel, outs, scratch, args, scalar=False):
    whole = pl.BlockSpec(memory_space=pltpu.VMEM)
    specs = [whole for _ in args]
    if scalar:
        specs[0] = pl.BlockSpec(memory_space=pltpu.SMEM)
    return pl.pallas_call(
        kernel,
        out_shape=[jax.ShapeDtypeStruct(shape, dtype) for shape, dtype in outs],
        in_specs=specs,
        out_specs=[whole for _ in outs],
        scratch_shapes=[pltpu.VMEM(shape, dtype) for shape, dtype in scratch],
        compiler_params=pltpu.CompilerParams(vmem_limit_bytes=40 << 20),
        cost_estimate=pl.CostEstimate(flops=1 << 28, bytes_accessed=4 << 20, transcendentals=0),
    )(*args)


def _first(*args):
    def whole(shape):
        return pl.BlockSpec(shape, lambda i: (0,) * len(shape))

    in_specs = [whole(arg.shape) for arg in args]
    in_specs[3] = pl.BlockSpec((1, 128, 512), lambda i: (0, 0, 0))
    return pl.pallas_call(
        _first_kernel,
        grid=(1,),
        out_shape=jax.ShapeDtypeStruct((4096, 128), BF16),
        in_specs=in_specs,
        out_specs=whole((4096, 128)),
        scratch_shapes=[pltpu.VMEM(*OPERAND_SCRATCH)],
        compiler_params=pltpu.CompilerParams(vmem_limit_bytes=60 << 20),
    )(*args)


def _exchange(tiles, group):
    return lax.all_to_all(tiles, group, split_axis=0, concat_axis=0, tiled=True)


def _products(kernel, group, sources, scratch, tiles):
    own = _exchange(tiles.reshape(128, 32, 128), group).reshape(*sources, 2, 16, 128)
    other = lax.ppermute(own, "core", [(0, 1), (1, 0)])
    core = lax.axis_index("core").astype(jnp.int32).reshape(1)
    (out,) = _call(
        kernel, [((16, 16, 16, 128), BF16)], scratch, (core, own, other), scalar=True
    )
    return _exchange(out.reshape(256, 16, 128), ("zhi", "yhi", "ylo", "zlo", "xhi", "xlo"))


def body(pair_rep, in_gain, in_bias, proj_w, gate_w, out_gain, out_bias, out_w):
    turned = (16, 128, 128)
    tiles = _first(pair_rep, in_gain, in_bias, proj_w)
    tiles, again = lax.optimization_barrier((tiles, pair_rep))
    gate, cells, columns = _call(
        _first_gate_kernel,
        [(turned, F32), (turned, BF16), ((6, 128, 128), F32)],
        [],
        (again, in_gain, in_bias, gate_w, out_gain, out_bias),
    )
    tri = _products(
        _outgoing_kernel,
        OUTGOING,
        (16, 8),
        [((16, 2, 16, 512), BF16), ((16, 2, 2, 16, 512), BF16)],
        tiles,
    ).reshape(64, 2, 2, 16, 128)
    middle, tiles = _call(
        _middle_kernel,
        [(turned, BF16), ((4096, 128), BF16)],
        [PRODUCT_SCRATCH, OPERAND_SCRATCH],
        (tri, cells, gate, columns, out_w, proj_w),
    )
    (gate,) = _call(_middle_gate_kernel, [(turned, F32)], [], (middle, columns, gate_w))
    tri = _products(
        _incoming_kernel,
        INCOMING,
        (8, 16),
        [((2, 2, 8, 16, 512), BF16), ((2, 2, 8, 16, 1024), BF16)],
        tiles,
    ).reshape(2, 2, 64, 16, 128)
    (out,) = _call(
        _last_kernel,
        [(pair_rep.shape, BF16)],
        [PRODUCT_SCRATCH],
        (tri, middle, gate, columns, out_w),
    )
    return out


def solution(mesh):
    fine = Mesh(
        mesh.devices.reshape(2, 2, 4, 2, 4, 2, 2),
        ("zhi", "yhi", "ylo", "core", "zlo", "xhi", "xlo"),
    )
    cells = P(("zhi", "yhi", "ylo", "core"), ("zlo", "xhi", "xlo"), None)
    placed = (cells, P(), P(), P(), P(), P(), P(), P())
    return jax.shard_map(body, mesh=fine, in_specs=placed, out_specs=cells, check_vma=False)
```

```python
import functools

import jax
import jax.numpy as jnp
from jax import lax
from jax.experimental import pallas as pl
from jax.experimental.pallas import tpu as pltpu
from jax.sharding import Mesh
from jax.sharding import PartitionSpec as P

OUTGOING = ("zhi", "yhi", "ylo", "zlo", "xlo")
INCOMING = ("zhi", "ylo", "zlo", "xhi", "xlo")
EPS = 1e-05
F32 = jnp.float32
BF16 = jnp.bfloat16

OPERAND_STEP = 40
PRODUCT_STEP = 24
OPERAND_SCRATCH = ((129 * OPERAND_STEP, 128), F32)
PRODUCT_SCRATCH = ((129 * PRODUCT_STEP, 128), F32)


def _norm(values, gain, bias):
    center = values - jnp.mean(values, axis=0, keepdims=True)
    spread = jnp.mean(center * center, axis=0, keepdims=True)
    return (center * lax.rsqrt(spread + EPS) * gain + bias).astype(BF16)


def _column(row):
    return jnp.broadcast_to(row, (128, 128)).T


def _beside(one, two):
    return jnp.concatenate([one, two], axis=1)


def _twice(one):
    return _beside(one, one)


def _put_two(ref, s, value):
    ref[s] = value[:, :128]
    ref[s + 1] = value[:, 128:]


def _project(cells, gain, bias, turned_w, scr, s):
    normed = _norm(cells.astype(F32), gain, bias)
    halves = jnp.dot(turned_w, normed, preferred_element_type=F32)
    left = jax.nn.sigmoid(halves[128:256]) * halves[:128]
    right = jax.nn.sigmoid(halves[384:]) * halves[256:384]
    for i in range(2):
        lanes = slice(128 * i, 128 * i + 128)
        scr[pl.ds(s + i, 128, stride=OPERAND_STEP), :] = left[:, lanes]
        scr[pl.ds(16 + s + i, 128, stride=OPERAND_STEP), :] = right[:, lanes]


def _gate(cells, gain, bias, turned_gate_w):
    normed = _norm(cells.astype(F32), gain, bias)
    return jax.nn.sigmoid(jnp.dot(turned_gate_w, normed, preferred_element_type=F32))


def _put_operands(out_ref, scr):
    rows = scr[: 128 * OPERAND_STEP].reshape(128, OPERAND_STEP, 128)[:, :32]
    out_ref[...] = rows.astype(BF16).reshape(4096, 128)


def _turned_rows(p_ref, s):
    return jnp.concatenate([p_ref[s], p_ref[16 + s]], axis=0).T


def _first_kernel(p_ref, gain_ref, bias_ref, w_ref, out_ref, scr):
    turned_w = w_ref[0].T
    gain, bias = _twice(_column(gain_ref[:1])), _twice(_column(bias_ref[:1]))
    for s in range(0, 16, 2):
        cells = _beside(_turned_rows(p_ref, s), _turned_rows(p_ref, s + 1))
        _project(cells, gain, bias, turned_w, scr, s)
    _put_operands(out_ref, scr)


def _first_gate_kernel(
    p_ref, gain_ref, bias_ref, gw_ref, og_ref, ob_ref, gate_ref, turned_ref, columns_ref
):
    turned_gate_w = gw_ref[0].T
    gain, bias = _twice(_column(gain_ref[:1])), _twice(_column(bias_ref[:1]))
    for s in range(0, 16, 2):
        cells = _beside(_turned_rows(p_ref, s), _turned_rows(p_ref, s + 1))
        _put_two(turned_ref, s, cells)
        _put_two(gate_ref, s, _gate(cells, gain, bias, turned_gate_w))
    columns_ref[0] = _column(gain_ref[1:])
    columns_ref[1] = _column(bias_ref[1:])
    for u in range(2):
        columns_ref[2 + 2 * u] = _column(og_ref[u : u + 1])
        columns_ref[3 + 2 * u] = _column(ob_ref[u : u + 1])


def _middle_gate_kernel(p_ref, columns_ref, gw_ref, gate_ref):
    turned_gate_w = gw_ref[1].T
    gain, bias = (_twice(columns_ref[i]) for i in range(2))
    for s in range(0, 16, 2):
        cells = _beside(p_ref[s], p_ref[s + 1])
        _put_two(gate_ref, s, _gate(cells, gain, bias, turned_gate_w))


def _load_products(one, two, scr):
    total = (one.astype(F32) + two.astype(F32)).reshape(128, 16, 128)
    for c in range(128):
        scr[c * PRODUCT_STEP : c * PRODUCT_STEP + 16, :] = total[c]


def _finished(scr, s, p_ref, g_ref, gain, bias, turned_w):
    tri = _beside(
        scr[pl.ds(s, 128, stride=PRODUCT_STEP), :], scr[pl.ds(s + 1, 128, stride=PRODUCT_STEP), :]
    )
    mixed = _norm(tri, gain, bias)
    projected = jnp.dot(turned_w, mixed, preferred_element_type=F32)
    cells = _beside(p_ref[s], p_ref[s + 1]).astype(F32)
    return (cells + _beside(g_ref[s], g_ref[s + 1]) * projected).astype(BF16)


def _middle_kernel(
    t_ref, p_ref, g_ref, columns_ref, ow_ref, w_ref, mid_ref, out_ref, tri_scr, scr
):
    _load_products(t_ref[:, 0], t_ref[:, 1], tri_scr)
    turned_w, turned_out_w = w_ref[1].T, ow_ref[0].T
    gain, bias, out_gain, out_bias = (_twice(columns_ref[i]) for i in range(4))
    for s in range(0, 16, 2):
        mid = _finished(tri_scr, s, p_ref, g_ref, out_gain, out_bias, turned_out_w)
        _put_two(mid_ref, s, mid)
    for s in range(0, 16, 2):
        _project(_beside(mid_ref[s], mid_ref[s + 1]), gain, bias, turned_w, scr, s)
    _put_operands(out_ref, scr)


def _last_kernel(t_ref, p_ref, g_ref, columns_ref, ow_ref, out_ref, tri_scr):
    _load_products(t_ref[:, 0], t_ref[:, 1], tri_scr)
    turned_w = ow_ref[1].T
    gain, bias = _twice(columns_ref[4]), _twice(columns_ref[5])
    for s in range(0, 16, 2):
        out = _finished(tri_scr, s, p_ref, g_ref, gain, bias, turned_w).T
        out_ref[s] = out[:64]
        out_ref[16 + s] = out[64:128]
        out_ref[s + 1] = out[128:192]
        out_ref[17 + s] = out[192:]


def _pair_up(one, two):
    low = jnp.concatenate([one[..., :64], two[..., :64]], axis=-1)
    high = jnp.concatenate([one[..., 64:], two[..., 64:]], axis=-1)
    return low, high


def _quarter(parts, q):
    return jnp.concatenate([part[..., 32 * q : 32 * q + 32] for part in parts], axis=-1)


def _put_products(out_ref, rows, tri):
    tri = tri.astype(BF16).reshape(-1, 2, 16, 1024)
    for pair in range(8):
        lanes = tri[..., pair * 128 : pair * 128 + 128]
        low, high = _pair_up(lanes[:, 0], lanes[:, 1])
        out_ref[rows, 2 * pair] = low
        out_ref[rows, 2 * pair + 1] = high


def _outgoing_kernel(core_ref, own_ref, other_ref, out_ref, l_scr, r_scr):
    core = core_ref[0]
    for pair in range(4):
        lanes = slice(pair * 128, pair * 128 + 128)
        left = _pair_up(own_ref[:, 2 * pair, 0], own_ref[:, 2 * pair + 1, 0])
        right = _pair_up(own_ref[:, 2 * pair, 1], own_ref[:, 2 * pair + 1, 1])
        away = _pair_up(other_ref[:, 2 * pair, 1], other_ref[:, 2 * pair + 1, 1])
        for b in range(2):
            l_scr[:, b, :, lanes] = left[b]
            r_scr[:, pl.ds(core, 1), b, :, lanes] = right[b][:, None]
            r_scr[:, pl.ds(1 - core, 1), b, :, lanes] = away[b][:, None]
    right = r_scr[...].reshape(1024, 512)
    for part in range(2):
        rows = slice(part * 8, part * 8 + 8)
        left = l_scr[rows].reshape(256, 512)
        tri = lax.dot_general(left, right, (((1,), (1,)), ((), ())), preferred_element_type=F32)
        _put_products(out_ref, rows, tri)


def _incoming_kernel(core_ref, own_ref, other_ref, out_ref, l_scr, r_scr):
    def load_left(core):
        for at, ref in ((0, own_ref), (1, other_ref)):
            for zlo in range(4):
                parts = [ref[:, zlo * 4 + x, 0] for x in range(4)]
                lanes = slice(zlo * 128, zlo * 128 + 128)
                for b in range(2):
                    l_scr[at, b, :, :, lanes] = _quarter(parts, 2 * b + core)

    for core in range(2):
        pl.when(core_ref[0] == core)(functools.partial(load_left, core))
    for at, ref in ((0, own_ref), (1, other_ref)):
        for pair in range(8):
            lanes = slice(pair * 128, pair * 128 + 128)
            right = _pair_up(ref[:, 2 * pair, 1], ref[:, 2 * pair + 1, 1])
            for b in range(2):
                r_scr[at, b, :, :, lanes] = right[b]
    right = r_scr[...].reshape(512, 1024)
    for part in range(2):
        left = l_scr[:, :, :, :, part * 256 : part * 256 + 256].reshape(512, 256)
        tri = lax.dot_general(left, right, (((0,), (0,)), ((), ())), preferred_element_type=F32)
        _put_products(out_ref, slice(part * 8, part * 8 + 8), tri)


def _call(kernel, outs, scratch, args, scalar=False):
    whole = pl.BlockSpec(memory_space=pltpu.VMEM)
    specs = [whole for _ in args]
    if scalar:
        specs[0] = pl.BlockSpec(memory_space=pltpu.SMEM)
    return pl.pallas_call(
        kernel,
        out_shape=[jax.ShapeDtypeStruct(shape, dtype) for shape, dtype in outs],
        in_specs=specs,
        out_specs=[whole for _ in outs],
        scratch_shapes=[pltpu.VMEM(shape, dtype) for shape, dtype in scratch],
        compiler_params=pltpu.CompilerParams(vmem_limit_bytes=40 << 20),
        cost_estimate=pl.CostEstimate(flops=1 << 28, bytes_accessed=4 << 20, transcendentals=0),
    )(*args)


def _first(*args):
    def whole(shape):
        return pl.BlockSpec(shape, lambda i: (0,) * len(shape))

    in_specs = [whole(arg.shape) for arg in args]
    in_specs[3] = pl.BlockSpec((1, 128, 512), lambda i: (0, 0, 0))
    return pl.pallas_call(
        _first_kernel,
        grid=(1,),
        out_shape=jax.ShapeDtypeStruct((4096, 128), BF16),
        in_specs=in_specs,
        out_specs=whole((4096, 128)),
        scratch_shapes=[pltpu.VMEM(*OPERAND_SCRATCH)],
        compiler_params=pltpu.CompilerParams(vmem_limit_bytes=60 << 20),
    )(*args)


def _exchange(tiles, group):
    return lax.all_to_all(tiles, group, split_axis=0, concat_axis=0, tiled=True)


def _operands(tiles, group, sources):
    return _exchange(tiles.reshape(128, 32, 128), group).reshape(*sources, 2, 16, 128)


def _products(kernel, scratch, own, gate):
    other = lax.ppermute(own, "core", [(0, 1), (1, 0)])
    other, gate = lax.optimization_barrier((other, gate))
    core = lax.axis_index("core").astype(jnp.int32).reshape(1)
    (out,) = _call(
        kernel, [((16, 16, 16, 128), BF16)], scratch, (core, own, other), scalar=True
    )
    return _exchange(out.reshape(256, 16, 128), ("zhi", "yhi", "ylo", "zlo", "xhi", "xlo")), gate


def body(pair_rep, in_gain, in_bias, proj_w, gate_w, out_gain, out_bias, out_w):
    turned = (16, 128, 128)
    tiles = _first(pair_rep, in_gain, in_bias, proj_w)
    tiles, again = lax.optimization_barrier((tiles, pair_rep))
    gate, cells, columns = _call(
        _first_gate_kernel,
        [(turned, F32), (turned, BF16), ((6, 128, 128), F32)],
        [],
        (again, in_gain, in_bias, gate_w, out_gain, out_bias),
    )
    tri, gate = _products(
        _outgoing_kernel,
        [((16, 2, 16, 512), BF16), ((16, 2, 2, 16, 512), BF16)],
        _operands(tiles, OUTGOING, (16, 8)),
        gate,
    )
    tri = tri.reshape(64, 2, 2, 16, 128)
    middle, tiles = _call(
        _middle_kernel,
        [(turned, BF16), ((4096, 128), BF16)],
        [PRODUCT_SCRATCH, OPERAND_SCRATCH],
        (tri, cells, gate, columns, out_w, proj_w),
    )
    own, again = lax.optimization_barrier((_operands(tiles, INCOMING, (8, 16)), middle))
    (gate,) = _call(_middle_gate_kernel, [(turned, F32)], [], (again, columns, gate_w))
    tri, gate = _products(
        _incoming_kernel,
        [((2, 2, 8, 16, 512), BF16), ((2, 2, 8, 16, 1024), BF16)],
        own,
        gate,
    )
    tri = tri.reshape(2, 2, 64, 16, 128)
    (out,) = _call(
        _last_kernel,
        [(pair_rep.shape, BF16)],
        [PRODUCT_SCRATCH],
        (tri, middle, gate, columns, out_w),
    )
    return out


def solution(mesh):
    fine = Mesh(
        mesh.devices.reshape(2, 2, 4, 2, 4, 2, 2),
        ("zhi", "yhi", "ylo", "core", "zlo", "xhi", "xlo"),
    )
    cells = P(("zhi", "yhi", "ylo", "core"), ("zlo", "xhi", "xlo"), None)
    placed = (cells, P(), P(), P(), P(), P(), P(), P())
    return jax.shard_map(body, mesh=fine, in_specs=placed, out_specs=cells, check_vma=False)
```

```python
import functools

import jax
import jax.numpy as jnp
from jax import lax
from jax.experimental import pallas as pl
from jax.experimental.pallas import tpu as pltpu
from jax.sharding import Mesh
from jax.sharding import PartitionSpec as P

OUTGOING = ("zhi", "yhi", "ylo", "zlo", "xlo")
INCOMING = ("zhi", "ylo", "zlo", "xhi", "xlo")
EPS = 1e-05
F32 = jnp.float32
BF16 = jnp.bfloat16

OPERAND_STEP = 40
PRODUCT_STEP = 24
OPERAND_SCRATCH = ((129 * OPERAND_STEP, 128), F32)
PRODUCT_SCRATCH = ((129 * PRODUCT_STEP, 128), F32)


def _norm(values, gain, bias):
    center = values - jnp.mean(values, axis=0, keepdims=True)
    spread = jnp.mean(center * center, axis=0, keepdims=True)
    return (center * lax.rsqrt(spread + EPS) * gain + bias).astype(BF16)


def _column(row):
    return jnp.broadcast_to(row, (128, 128)).T


def _beside(one, two):
    return jnp.concatenate([one, two], axis=1)


def _twice(one):
    return _beside(one, one)


def _put_two(ref, s, value):
    ref[s] = value[:, :128]
    ref[s + 1] = value[:, 128:]


def _project(cells, gain, bias, turned_w, scr, s):
    normed = _norm(cells.astype(F32), gain, bias)
    halves = jnp.dot(turned_w, normed, preferred_element_type=F32)
    left = jax.nn.sigmoid(halves[128:256]) * halves[:128]
    right = jax.nn.sigmoid(halves[384:]) * halves[256:384]
    for i in range(2):
        lanes = slice(128 * i, 128 * i + 128)
        scr[pl.ds(s + i, 128, stride=OPERAND_STEP), :] = left[:, lanes]
        scr[pl.ds(16 + s + i, 128, stride=OPERAND_STEP), :] = right[:, lanes]


def _gate(cells, gain, bias, turned_gate_w):
    normed = _norm(cells.astype(F32), gain, bias)
    return jax.nn.sigmoid(jnp.dot(turned_gate_w, normed, preferred_element_type=F32))


def _put_operands(out_ref, scr):
    rows = scr[: 128 * OPERAND_STEP].reshape(128, OPERAND_STEP, 128)[:, :32]
    out_ref[...] = rows.astype(BF16).reshape(4096, 128)


def _turned_rows(p_ref, s):
    return jnp.concatenate([p_ref[s], p_ref[16 + s]], axis=0).T


def _first_kernel(p_ref, gain_ref, bias_ref, w_ref, out_ref, scr):
    turned_w = w_ref[0].T
    gain, bias = _twice(_column(gain_ref[:1])), _twice(_column(bias_ref[:1]))
    for s in range(0, 16, 2):
        cells = _beside(_turned_rows(p_ref, s), _turned_rows(p_ref, s + 1))
        _project(cells, gain, bias, turned_w, scr, s)
    _put_operands(out_ref, scr)


def _first_gate_kernel(
    p_ref, gain_ref, bias_ref, gw_ref, og_ref, ob_ref, gate_ref, turned_ref, columns_ref
):
    turned_gate_w = gw_ref[0].T
    gain, bias = _twice(_column(gain_ref[:1])), _twice(_column(bias_ref[:1]))
    for s in range(0, 16, 2):
        cells = _beside(_turned_rows(p_ref, s), _turned_rows(p_ref, s + 1))
        _put_two(turned_ref, s, cells)
        _put_two(gate_ref, s, _gate(cells, gain, bias, turned_gate_w))
    columns_ref[0] = _column(gain_ref[1:])
    columns_ref[1] = _column(bias_ref[1:])
    for u in range(2):
        columns_ref[2 + 2 * u] = _column(og_ref[u : u + 1])
        columns_ref[3 + 2 * u] = _column(ob_ref[u : u + 1])


def _middle_gate_kernel(p_ref, columns_ref, gw_ref, gate_ref):
    turned_gate_w = gw_ref[1].T
    gain, bias = (_twice(columns_ref[i]) for i in range(2))
    for s in range(0, 16, 2):
        cells = _beside(p_ref[s], p_ref[s + 1])
        _put_two(gate_ref, s, _gate(cells, gain, bias, turned_gate_w))


def _load_products(one, two, scr):
    total = (one.astype(F32) + two.astype(F32)).reshape(128, 16, 128)
    for c in range(128):
        scr[c * PRODUCT_STEP : c * PRODUCT_STEP + 16, :] = total[c]


def _finished(scr, s, p_ref, g_ref, gain, bias, turned_w):
    tri = _beside(
        scr[pl.ds(s, 128, stride=PRODUCT_STEP), :], scr[pl.ds(s + 1, 128, stride=PRODUCT_STEP), :]
    )
    mixed = _norm(tri, gain, bias)
    projected = jnp.dot(turned_w, mixed, preferred_element_type=F32)
    cells = _beside(p_ref[s], p_ref[s + 1]).astype(F32)
    return (cells + _beside(g_ref[s], g_ref[s + 1]) * projected).astype(BF16)


def _middle_kernel(
    t_ref, p_ref, g_ref, columns_ref, ow_ref, w_ref, mid_ref, out_ref, tri_scr, scr
):
    _load_products(t_ref[:, 0], t_ref[:, 1], tri_scr)
    turned_w, turned_out_w = w_ref[1].T, ow_ref[0].T
    gain, bias, out_gain, out_bias = (_twice(columns_ref[i]) for i in range(4))
    for s in range(0, 16, 2):
        mid = _finished(tri_scr, s, p_ref, g_ref, out_gain, out_bias, turned_out_w)
        _put_two(mid_ref, s, mid)
    for s in range(0, 16, 2):
        _project(_beside(mid_ref[s], mid_ref[s + 1]), gain, bias, turned_w, scr, s)
    _put_operands(out_ref, scr)


def _last_kernel(t_ref, p_ref, g_ref, columns_ref, ow_ref, out_ref, tri_scr):
    _load_products(t_ref[:, 0], t_ref[:, 1], tri_scr)
    turned_w = ow_ref[1].T
    gain, bias = _twice(columns_ref[4]), _twice(columns_ref[5])
    for s in range(0, 16, 2):
        out = _finished(tri_scr, s, p_ref, g_ref, gain, bias, turned_w).T
        out_ref[s] = out[:64]
        out_ref[16 + s] = out[64:128]
        out_ref[s + 1] = out[128:192]
        out_ref[17 + s] = out[192:]


def _pair_up(one, two):
    low = jnp.concatenate([one[..., :64], two[..., :64]], axis=-1)
    high = jnp.concatenate([one[..., 64:], two[..., 64:]], axis=-1)
    return low, high


def _quarter(parts, q):
    return jnp.concatenate([part[..., 32 * q : 32 * q + 32] for part in parts], axis=-1)


def _put_products(out_ref, rows, tri):
    tri = tri.astype(BF16).reshape(-1, 2, 16, 1024)
    for pair in range(8):
        lanes = tri[..., pair * 128 : pair * 128 + 128]
        low, high = _pair_up(lanes[:, 0], lanes[:, 1])
        out_ref[rows, 2 * pair] = low
        out_ref[rows, 2 * pair + 1] = high


def _outgoing_kernel(core_ref, own_ref, other_ref, out_ref, l_scr, r_scr):
    core = core_ref[0]
    for pair in range(4):
        lanes = slice(pair * 128, pair * 128 + 128)
        left = _pair_up(own_ref[:, 2 * pair, 0], own_ref[:, 2 * pair + 1, 0])
        right = _pair_up(own_ref[:, 2 * pair, 1], own_ref[:, 2 * pair + 1, 1])
        away = _pair_up(other_ref[:, 2 * pair, 1], other_ref[:, 2 * pair + 1, 1])
        for b in range(2):
            l_scr[:, b, :, lanes] = left[b]
            r_scr[:, pl.ds(core, 1), b, :, lanes] = right[b][:, None]
            r_scr[:, pl.ds(1 - core, 1), b, :, lanes] = away[b][:, None]
    right = r_scr[...].reshape(1024, 512)
    for part in range(2):
        rows = slice(part * 8, part * 8 + 8)
        left = l_scr[rows].reshape(256, 512)
        tri = lax.dot_general(left, right, (((1,), (1,)), ((), ())), preferred_element_type=F32)
        _put_products(out_ref, rows, tri)


def _incoming_rows(core_ref, ref, l_ref, r_ref):
    def load_left(core):
        for zlo in range(4):
            parts = [ref[:, zlo * 4 + x, 0] for x in range(4)]
            lanes = slice(zlo * 128, zlo * 128 + 128)
            for b in range(2):
                l_ref[b, :, :, lanes] = _quarter(parts, 2 * b + core)

    for core in range(2):
        pl.when(core_ref[0] == core)(functools.partial(load_left, core))
    for pair in range(8):
        lanes = slice(pair * 128, pair * 128 + 128)
        right = _pair_up(ref[:, 2 * pair, 1], ref[:, 2 * pair + 1, 1])
        for b in range(2):
            r_ref[b, :, :, lanes] = right[b]


def _incoming_kernel(core_ref, other_ref, l_own, r_own, out_ref, l_scr, r_scr):
    _incoming_rows(core_ref, other_ref, l_scr, r_scr)
    rights = r_own[...].reshape(256, 1024), r_scr[...].reshape(256, 1024)
    for part in range(2):
        lanes = slice(part * 256, part * 256 + 256)
        lefts = l_own[:, :, :, lanes].reshape(256, 256), l_scr[:, :, :, lanes].reshape(256, 256)
        tri = lax.dot_general(
            jnp.concatenate(lefts, axis=0),
            jnp.concatenate(rights, axis=0),
            (((0,), (0,)), ((), ())),
            preferred_element_type=F32,
        )
        _put_products(out_ref, slice(part * 8, part * 8 + 8), tri)


def _call(kernel, outs, scratch, args, scalar=False):
    whole = pl.BlockSpec(memory_space=pltpu.VMEM)
    specs = [whole for _ in args]
    if scalar:
        specs[0] = pl.BlockSpec(memory_space=pltpu.SMEM)
    return pl.pallas_call(
        kernel,
        out_shape=[jax.ShapeDtypeStruct(shape, dtype) for shape, dtype in outs],
        in_specs=specs,
        out_specs=[whole for _ in outs],
        scratch_shapes=[pltpu.VMEM(shape, dtype) for shape, dtype in scratch],
        compiler_params=pltpu.CompilerParams(vmem_limit_bytes=40 << 20),
        cost_estimate=pl.CostEstimate(flops=1 << 28, bytes_accessed=4 << 20, transcendentals=0),
    )(*args)


def _first(*args):
    def whole(shape):
        return pl.BlockSpec(shape, lambda i: (0,) * len(shape))

    in_specs = [whole(arg.shape) for arg in args]
    in_specs[3] = pl.BlockSpec((1, 128, 512), lambda i: (0, 0, 0))
    return pl.pallas_call(
        _first_kernel,
        grid=(1,),
        out_shape=jax.ShapeDtypeStruct((4096, 128), BF16),
        in_specs=in_specs,
        out_specs=whole((4096, 128)),
        scratch_shapes=[pltpu.VMEM(*OPERAND_SCRATCH)],
        compiler_params=pltpu.CompilerParams(vmem_limit_bytes=60 << 20),
    )(*args)


def _exchange(tiles, group):
    return lax.all_to_all(tiles, group, split_axis=0, concat_axis=0, tiled=True)


def _operands(tiles, group, sources):
    return _exchange(tiles.reshape(128, 32, 128), group).reshape(*sources, 2, 16, 128)


def _core():
    return lax.axis_index("core").astype(jnp.int32).reshape(1)


def _swap(own, *made):
    other = lax.ppermute(own, "core", [(0, 1), (1, 0)])
    return lax.optimization_barrier((other, *made))


def _products(kernel, scratch, *args):
    (out,) = _call(kernel, [((16, 16, 16, 128), BF16)], scratch, (_core(), *args), scalar=True)
    return _exchange(out.reshape(256, 16, 128), ("zhi", "yhi", "ylo", "zlo", "xhi", "xlo"))


def body(pair_rep, in_gain, in_bias, proj_w, gate_w, out_gain, out_bias, out_w):
    turned = (16, 128, 128)
    tiles = _first(pair_rep, in_gain, in_bias, proj_w)
    tiles, again = lax.optimization_barrier((tiles, pair_rep))
    gate, cells, columns = _call(
        _first_gate_kernel,
        [(turned, F32), (turned, BF16), ((6, 128, 128), F32)],
        [],
        (again, in_gain, in_bias, gate_w, out_gain, out_bias),
    )
    own = _operands(tiles, OUTGOING, (16, 8))
    other, gate = _swap(own, gate)
    tri = _products(
        _outgoing_kernel,
        [((16, 2, 16, 512), BF16), ((16, 2, 2, 16, 512), BF16)],
        own,
        other,
    ).reshape(64, 2, 2, 16, 128)
    middle, tiles = _call(
        _middle_kernel,
        [(turned, BF16), ((4096, 128), BF16)],
        [PRODUCT_SCRATCH, OPERAND_SCRATCH],
        (tri, cells, gate, columns, out_w, proj_w),
    )
    own, again = lax.optimization_barrier((_operands(tiles, INCOMING, (8, 16)), middle))
    (gate,) = _call(_middle_gate_kernel, [(turned, F32)], [], (again, columns, gate_w))
    rows = [((2, 8, 16, 512), BF16), ((2, 8, 16, 1024), BF16)]
    left, right = _call(_incoming_rows, rows, [], (_core(), own), scalar=True)
    other, gate, left, right = _swap(own, gate, left, right)
    tri = _products(_incoming_kernel, rows, other, left, right).reshape(2, 2, 64, 16, 128)
    (out,) = _call(
        _last_kernel,
        [(pair_rep.shape, BF16)],
        [PRODUCT_SCRATCH],
        (tri, middle, gate, columns, out_w),
    )
    return out


def solution(mesh):
    fine = Mesh(
        mesh.devices.reshape(2, 2, 4, 2, 4, 2, 2),
        ("zhi", "yhi", "ylo", "core", "zlo", "xhi", "xlo"),
    )
    cells = P(("zhi", "yhi", "ylo", "core"), ("zlo", "xhi", "xlo"), None)
    placed = (cells, P(), P(), P(), P(), P(), P(), P())
    return jax.shard_map(body, mesh=fine, in_specs=placed, out_specs=cells, check_vma=False)
```

```python
import functools

import jax
import jax.numpy as jnp
from jax import lax
from jax.experimental import pallas as pl
from jax.experimental.pallas import tpu as pltpu
from jax.sharding import Mesh
from jax.sharding import PartitionSpec as P

OUTGOING = ("zhi", "yhi", "ylo", "zlo", "xlo")
INCOMING = ("zhi", "ylo", "zlo", "xhi", "xlo")
EPS = 1e-05
F32 = jnp.float32
BF16 = jnp.bfloat16

OPERAND_STEP = 40
PRODUCT_STEP = 24
OPERAND_SCRATCH = ((129 * OPERAND_STEP, 128), F32)
PRODUCT_SCRATCH = ((129 * PRODUCT_STEP, 128), F32)


def _norm(values, gain, bias):
    center = values - jnp.mean(values, axis=0, keepdims=True)
    spread = jnp.mean(center * center, axis=0, keepdims=True)
    return (center * lax.rsqrt(spread + EPS) * gain + bias).astype(BF16)


def _column(row):
    return jnp.broadcast_to(row, (128, 128)).T


def _beside(one, two):
    return jnp.concatenate([one, two], axis=1)


def _twice(one):
    return _beside(one, one)


def _put_two(ref, s, value):
    ref[s] = value[:, :128]
    ref[s + 1] = value[:, 128:]


def _project(cells, gain, bias, turned_w, scr, s):
    normed = _norm(cells.astype(F32), gain, bias)
    halves = jnp.dot(turned_w, normed, preferred_element_type=F32)
    left = jax.nn.sigmoid(halves[128:256]) * halves[:128]
    right = jax.nn.sigmoid(halves[384:]) * halves[256:384]
    for i in range(2):
        lanes = slice(128 * i, 128 * i + 128)
        scr[pl.ds(s + i, 128, stride=OPERAND_STEP), :] = left[:, lanes]
        scr[pl.ds(16 + s + i, 128, stride=OPERAND_STEP), :] = right[:, lanes]


def _gate(cells, gain, bias, turned_gate_w):
    normed = _norm(cells.astype(F32), gain, bias)
    return jax.nn.sigmoid(jnp.dot(turned_gate_w, normed, preferred_element_type=F32))


def _put_operands(out_ref, scr):
    rows = scr[: 128 * OPERAND_STEP].reshape(128, OPERAND_STEP, 128)[:, :32]
    out_ref[...] = rows.astype(BF16).reshape(4096, 128)


def _turned_rows(p_ref, s):
    return jnp.concatenate([p_ref[s], p_ref[16 + s]], axis=0).T


def _first_kernel(p_ref, gain_ref, bias_ref, w_ref, out_ref, scr):
    turned_w = w_ref[0].T
    gain, bias = _twice(_column(gain_ref[:1])), _twice(_column(bias_ref[:1]))
    for s in range(0, 16, 2):
        cells = _beside(_turned_rows(p_ref, s), _turned_rows(p_ref, s + 1))
        _project(cells, gain, bias, turned_w, scr, s)
    _put_operands(out_ref, scr)


def _first_gate_kernel(
    p_ref, gain_ref, bias_ref, gw_ref, og_ref, ob_ref, gate_ref, turned_ref, columns_ref
):
    turned_gate_w = gw_ref[0].T
    gain, bias = _twice(_column(gain_ref[:1])), _twice(_column(bias_ref[:1]))
    for s in range(0, 16, 2):
        cells = _beside(_turned_rows(p_ref, s), _turned_rows(p_ref, s + 1))
        _put_two(turned_ref, s, cells)
        _put_two(gate_ref, s, _gate(cells, gain, bias, turned_gate_w))
    columns_ref[0] = _column(gain_ref[1:])
    columns_ref[1] = _column(bias_ref[1:])
    for u in range(2):
        columns_ref[2 + 2 * u] = _column(og_ref[u : u + 1])
        columns_ref[3 + 2 * u] = _column(ob_ref[u : u + 1])


def _middle_gate_kernel(p_ref, columns_ref, gw_ref, gate_ref):
    turned_gate_w = gw_ref[1].T
    gain, bias = (_twice(columns_ref[i]) for i in range(2))
    for s in range(0, 16, 2):
        cells = _beside(p_ref[s], p_ref[s + 1])
        _put_two(gate_ref, s, _gate(cells, gain, bias, turned_gate_w))


def _load_products(one, two, scr):
    total = (one.astype(F32) + two.astype(F32)).reshape(128, 16, 128)
    for c in range(128):
        scr[c * PRODUCT_STEP : c * PRODUCT_STEP + 16, :] = total[c]


def _finished(scr, s, p_ref, g_ref, gain, bias, turned_w):
    tri = _beside(
        scr[pl.ds(s, 128, stride=PRODUCT_STEP), :], scr[pl.ds(s + 1, 128, stride=PRODUCT_STEP), :]
    )
    mixed = _norm(tri, gain, bias)
    projected = jnp.dot(turned_w, mixed, preferred_element_type=F32)
    cells = _beside(p_ref[s], p_ref[s + 1]).astype(F32)
    return (cells + _beside(g_ref[s], g_ref[s + 1]) * projected).astype(BF16)


def _middle_kernel(
    t_ref, p_ref, g_ref, columns_ref, ow_ref, w_ref, mid_ref, out_ref, tri_scr, scr
):
    _load_products(t_ref[:, 0], t_ref[:, 1], tri_scr)
    turned_w, turned_out_w = w_ref[1].T, ow_ref[0].T
    gain, bias, out_gain, out_bias = (_twice(columns_ref[i]) for i in range(4))
    for s in range(0, 16, 2):
        mid = _finished(tri_scr, s, p_ref, g_ref, out_gain, out_bias, turned_out_w)
        _put_two(mid_ref, s, mid)
    for s in range(0, 16, 2):
        _project(_beside(mid_ref[s], mid_ref[s + 1]), gain, bias, turned_w, scr, s)
    _put_operands(out_ref, scr)


def _last_kernel(t_ref, p_ref, g_ref, columns_ref, ow_ref, out_ref, tri_scr):
    _load_products(t_ref[:, 0], t_ref[:, 1], tri_scr)
    turned_w = ow_ref[1].T
    gain, bias = _twice(columns_ref[4]), _twice(columns_ref[5])
    for s in range(0, 16, 2):
        out = _finished(tri_scr, s, p_ref, g_ref, gain, bias, turned_w).T
        out_ref[s] = out[:64]
        out_ref[16 + s] = out[64:128]
        out_ref[s + 1] = out[128:192]
        out_ref[17 + s] = out[192:]


def _pair_up(one, two):
    low = jnp.concatenate([one[..., :64], two[..., :64]], axis=-1)
    high = jnp.concatenate([one[..., 64:], two[..., 64:]], axis=-1)
    return low, high


def _quarter(parts, q):
    return jnp.concatenate([part[..., 32 * q : 32 * q + 32] for part in parts], axis=-1)


def _put_products(out_ref, rows, tri):
    tri = tri.astype(BF16).reshape(-1, 2, 16, 1024)
    for pair in range(8):
        lanes = tri[..., pair * 128 : pair * 128 + 128]
        low, high = _pair_up(lanes[:, 0], lanes[:, 1])
        out_ref[rows, 2 * pair] = low
        out_ref[rows, 2 * pair + 1] = high


def _outgoing_kernel(core_ref, own_ref, other_ref, out_ref, l_scr, r_scr):
    core = core_ref[0]
    for pair in range(4):
        lanes = slice(pair * 128, pair * 128 + 128)
        left = _pair_up(own_ref[:, 2 * pair, 0], own_ref[:, 2 * pair + 1, 0])
        right = _pair_up(own_ref[:, 2 * pair, 1], own_ref[:, 2 * pair + 1, 1])
        away = _pair_up(other_ref[:, 2 * pair, 1], other_ref[:, 2 * pair + 1, 1])
        for b in range(2):
            l_scr[:, b, :, lanes] = left[b]
            r_scr[:, pl.ds(core, 1), b, :, lanes] = right[b][:, None]
            r_scr[:, pl.ds(1 - core, 1), b, :, lanes] = away[b][:, None]
    right = r_scr[...].reshape(1024, 512)
    left = l_scr[...].reshape(512, 512)
    tri = lax.dot_general(left, right, (((1,), (1,)), ((), ())), preferred_element_type=F32)
    _put_products(out_ref, slice(0, 16), tri)


def _incoming_rows(core_ref, ref, l_ref, r_ref):
    def load_left(core):
        for zlo in range(4):
            parts = [ref[:, zlo * 4 + x, 0] for x in range(4)]
            lanes = slice(zlo * 128, zlo * 128 + 128)
            for b in range(2):
                l_ref[b, :, :, lanes] = _quarter(parts, 2 * b + core)

    for core in range(2):
        pl.when(core_ref[0] == core)(functools.partial(load_left, core))
    for pair in range(8):
        lanes = slice(pair * 128, pair * 128 + 128)
        right = _pair_up(ref[:, 2 * pair, 1], ref[:, 2 * pair + 1, 1])
        for b in range(2):
            r_ref[b, :, :, lanes] = right[b]


def _incoming_kernel(core_ref, other_ref, l_own, r_own, out_ref, l_scr, r_scr):
    _incoming_rows(core_ref, other_ref, l_scr, r_scr)
    rights = r_own[...].reshape(256, 1024), r_scr[...].reshape(256, 1024)
    for part in range(2):
        lanes = slice(part * 256, part * 256 + 256)
        lefts = l_own[:, :, :, lanes].reshape(256, 256), l_scr[:, :, :, lanes].reshape(256, 256)
        tri = lax.dot_general(
            jnp.concatenate(lefts, axis=0),
            jnp.concatenate(rights, axis=0),
            (((0,), (0,)), ((), ())),
            preferred_element_type=F32,
        )
        _put_products(out_ref, slice(part * 8, part * 8 + 8), tri)


def _call(kernel, outs, scratch, args, scalar=False):
    whole = pl.BlockSpec(memory_space=pltpu.VMEM)
    specs = [whole for _ in args]
    if scalar:
        specs[0] = pl.BlockSpec(memory_space=pltpu.SMEM)
    return pl.pallas_call(
        kernel,
        out_shape=[jax.ShapeDtypeStruct(shape, dtype) for shape, dtype in outs],
        in_specs=specs,
        out_specs=[whole for _ in outs],
        scratch_shapes=[pltpu.VMEM(shape, dtype) for shape, dtype in scratch],
        compiler_params=pltpu.CompilerParams(vmem_limit_bytes=40 << 20),
        cost_estimate=pl.CostEstimate(flops=1 << 28, bytes_accessed=4 << 20, transcendentals=0),
    )(*args)


def _first(*args):
    def whole(shape):
        return pl.BlockSpec(shape, lambda i: (0,) * len(shape))

    in_specs = [whole(arg.shape) for arg in args]
    in_specs[3] = pl.BlockSpec((1, 128, 512), lambda i: (0, 0, 0))
    return pl.pallas_call(
        _first_kernel,
        grid=(1,),
        out_shape=jax.ShapeDtypeStruct((4096, 128), BF16),
        in_specs=in_specs,
        out_specs=whole((4096, 128)),
        scratch_shapes=[pltpu.VMEM(*OPERAND_SCRATCH)],
        compiler_params=pltpu.CompilerParams(vmem_limit_bytes=60 << 20),
    )(*args)


def _exchange(tiles, group):
    return lax.all_to_all(tiles, group, split_axis=0, concat_axis=0, tiled=True)


def _operands(tiles, group, sources):
    return _exchange(tiles.reshape(128, 32, 128), group).reshape(*sources, 2, 16, 128)


def _core():
    return lax.axis_index("core").astype(jnp.int32).reshape(1)


def _swap(own, *made):
    other = lax.ppermute(own, "core", [(0, 1), (1, 0)])
    return lax.optimization_barrier((other, *made))


def _products(kernel, scratch, *args):
    (out,) = _call(kernel, [((16, 16, 16, 128), BF16)], scratch, (_core(), *args), scalar=True)
    return _exchange(out.reshape(256, 16, 128), ("zhi", "yhi", "ylo", "zlo", "xhi", "xlo"))


def body(pair_rep, in_gain, in_bias, proj_w, gate_w, out_gain, out_bias, out_w):
    turned = (16, 128, 128)
    tiles = _first(pair_rep, in_gain, in_bias, proj_w)
    tiles, again = lax.optimization_barrier((tiles, pair_rep))
    gate, cells, columns = _call(
        _first_gate_kernel,
        [(turned, F32), (turned, BF16), ((6, 128, 128), F32)],
        [],
        (again, in_gain, in_bias, gate_w, out_gain, out_bias),
    )
    own = _operands(tiles, OUTGOING, (16, 8))
    other, gate = _swap(own, gate)
    tri = _products(
        _outgoing_kernel,
        [((16, 2, 16, 512), BF16), ((16, 2, 2, 16, 512), BF16)],
        own,
        other,
    ).reshape(64, 2, 2, 16, 128)
    middle, tiles = _call(
        _middle_kernel,
        [(turned, BF16), ((4096, 128), BF16)],
        [PRODUCT_SCRATCH, OPERAND_SCRATCH],
        (tri, cells, gate, columns, out_w, proj_w),
    )
    own, again = lax.optimization_barrier((_operands(tiles, INCOMING, (8, 16)), middle))
    (gate,) = _call(_middle_gate_kernel, [(turned, F32)], [], (again, columns, gate_w))
    rows = [((2, 8, 16, 512), BF16), ((2, 8, 16, 1024), BF16)]
    left, right = _call(_incoming_rows, rows, [], (_core(), own), scalar=True)
    other, gate, left, right = _swap(own, gate, left, right)
    tri = _products(_incoming_kernel, rows, other, left, right).reshape(2, 2, 64, 16, 128)
    (out,) = _call(
        _last_kernel,
        [(pair_rep.shape, BF16)],
        [PRODUCT_SCRATCH],
        (tri, middle, gate, columns, out_w),
    )
    return out


def solution(mesh):
    fine = Mesh(
        mesh.devices.reshape(2, 2, 4, 2, 4, 2, 2),
        ("zhi", "yhi", "ylo", "core", "zlo", "xhi", "xlo"),
    )
    cells = P(("zhi", "yhi", "ylo", "core"), ("zlo", "xhi", "xlo"), None)
    placed = (cells, P(), P(), P(), P(), P(), P(), P())
    return jax.shard_map(body, mesh=fine, in_specs=placed, out_specs=cells, check_vma=False)
```
